512 devices in a mesh: gx: 4 (over z_lo), gy: 8 (over x, core), gz: 16 (over y, z_hi).
Axes of the slice: x: 4, y: 4, z: 16 (z_hi: 4, z_lo: 4; z = z_hi * 4 + z_lo), core: 2. Of those that a mesh axis runs over, the one named last changes fastest.
Arguments:
- final_adjoint: float32 [9, 56, 65536], P(None, None, ('gx', 'gy', 'gz')), may hold values from -6 to 6
- star_mats: float32 [3, 9, 9, 65536], P(None, None, None, ('gx', 'gy', 'gz')), may hold values from -6 to 6
- deriv_stiff: float32 [3, 56, 56], replicated, may hold values from -6 to 6
- volume_stiffness: float32 [3, 56, 56], replicated, may hold values from -0.21875 to 0.21875
- face_projection: float32 [4, 21, 56], replicated, may hold values from -0.75 to 0.75
- flux_local: float32 [4, 9, 9, 65536], P(None, None, None, ('gx', 'gy', 'gz')), may hold values from -0.875 to 0.875
- flux_across: float32 [4, 9, 9, 65536], P(None, None, None, ('gx', 'gy', 'gz')), may hold values from -0.875 to 0.875
- cluster: int32 [65536], P(('gx', 'gy', 'gz')), may hold values from 0 to 1, as said below
- partner: int32 [4, 65536], P(None, ('gx', 'gy', 'gz')), may hold values from 0 to 703, as said below
- send_slots: int32 [6, 16384], P(None, ('gx', 'gy', 'gz')), may hold values from 0 to 511, as said below
Outputs:
- initial_adjoint: float32 [9, 56, 65536], P(None, None, ('gx', 'gy', 'gz'))
The draws below stay inside these ranges and needn't reach their ends.
Inputs may be any that keep to these rules, and one draw needn't show every extreme that they name: At most 64 of a partition's elements have cluster 0, some partition has exactly 64, and every partition has at least three sixteenths of 128. `send_slots`: row d of a partition lists 32 distinct face slots c * 128 + e lying on its boundary toward direction d; no slot is in two rows. At most 16 slots of a row belong to cluster-0 elements, and some row of some partition has exactly 16. partner[c, e] = 512 + d * 32 + j exactly when send_slots[d, j] of the partition is c * 128 + e; every other slot's partner is another slot of the same partition below 512 whose partner is it.
All inputs are finite; a program needn't handle non-finite values.
Results may differ from the reference program's by a relative error of at most 0.0003.
Values sent between devices are 32-bit elements; how exact they have to be, the bound alone decides.
A program may use at most 64 MiB of HBM per device.

```python
import math
import jax
import jax.numpy as jnp
from jax import lax

FIELDS = 9
MODES = 56
FACE_MODES = 21
TERMS = 6
FINE_STEPS = 4
E_DEV = 128
ELEMS = 65536
N_GX = 4
N_GY = 8
N_GZ = 16


def shuffled_slots(key):
    return jax.random.permutation(key, E_DEV // 4)


def partition_topology(key, starred, star_side):
    members = E_DEV
    width = members // 4
    most = width // 2
    streams = jax.random.split(key, 6)
    fast_count = jax.random.randint(streams[0], (), members * 3 // 16, members // 2 + 1)
    fast_count = jnp.where(starred, members // 2, fast_count)
    ranking = jnp.zeros((members,), jnp.int32).at[jax.random.permutation(streams[1], members)].set(jnp.arange(members, dtype=jnp.int32))
    kinds = (ranking >= fast_count).astype(jnp.int32)
    mixing = jax.random.permutation(streams[2], 4 * members)
    sorted_faces = mixing[jnp.argsort(kinds[mixing % members], stable=True)]
    per_side = jax.random.randint(streams[3], (6,), most // 2, most + 1)
    per_side = jnp.where(starred & (jnp.arange(6) == star_side), most, per_side)
    fast_start = jnp.cumsum(per_side) - per_side
    slow_start = jnp.cumsum(width - per_side) - (width - per_side) + 4 * fast_count
    column = jnp.arange(width, dtype=jnp.int32)[None, :]
    fast_pick = jnp.clip(fast_start[:, None] + column, 0, 4 * members - 1)
    slow_pick = jnp.clip(slow_start[:, None] + column - per_side[:, None], 0, 4 * members - 1)
    chosen = jnp.where(column < per_side[:, None], sorted_faces[fast_pick], sorted_faces[slow_pick])
    shuffles = jax.vmap(shuffled_slots)(jax.random.split(streams[4], 6))
    listing = jnp.take_along_axis(chosen, shuffles, axis=1).astype(jnp.int32)
    flat_list = listing.reshape(-1)
    remote = jnp.zeros((4 * members,), jnp.int32).at[flat_list].set(1)
    scramble = jax.random.permutation(streams[5], 4 * members)
    lined = scramble[jnp.argsort(remote[scramble], stable=True)]
    paired = 4 * members - 6 * width
    first_side = lined[0:paired:2]
    second_side = lined[1:paired:2]
    links = jnp.zeros((4 * members,), jnp.int32).at[first_side].set(second_side).at[second_side].set(first_side)
    links = links.at[flat_list].set(4 * members + jnp.arange(6 * width, dtype=jnp.int32))
    return (kinds, links.reshape(4, members), listing)


def mesh_topology(key):
    base = jax.random.fold_in(key, 7)
    groups = ELEMS // E_DEV
    starred_group = jax.random.randint(jax.random.fold_in(base, 1), (), 0, groups)
    star_side = jax.random.randint(jax.random.fold_in(base, 2), (), 0, 6)
    group_keys = jax.random.split(jax.random.fold_in(base, 3), groups)
    marks = jnp.arange(groups) == starred_group
    kinds, links, listing = jax.vmap(partition_topology, in_axes=(0, 0, None))(group_keys, marks, star_side)
    kinds = kinds.reshape(-1)
    links = jnp.transpose(links, (1, 0, 2)).reshape(4, -1)
    listing = jnp.transpose(listing, (1, 0, 2)).reshape(6, -1)
    return (kinds, links, listing)


def draw_cluster(key, part):
    return mesh_topology(key)[0]


def draw_partner(key, part):
    return mesh_topology(key)[1]


def draw_send_slots(key, part):
    return mesh_topology(key)[2]


def draw_star_mats(key, part):
    kinds = mesh_topology(key)[0]
    speed = jnp.where(kinds == 0, 1.0, 0.25).astype(jnp.float32)
    inner = jax.random.fold_in(key, 11)
    raw = jax.random.truncated_normal(inner, -4.0, 4.0, (3, FIELDS, FIELDS, ELEMS), jnp.float32)
    return (raw + jnp.transpose(raw, (0, 2, 1, 3))) * (0.7 * speed)


def draw_deriv_stiff(key, part):
    inner = jax.random.fold_in(key, 13)
    raw = jax.random.truncated_normal(inner, -4.0, 4.0, (3, MODES, MODES), jnp.float32)
    return (raw - jnp.transpose(raw, (0, 2, 1))) * (0.7 / math.sqrt(MODES))


def block_scale(stream_key, dims, cuts, smallest, high):
    def one(dim, shards_of):
        draws = jax.random.uniform(jax.random.fold_in(jax.random.fold_in(stream_key, 6), dim), (shards_of,), jnp.float32, smallest / len(cuts), high / len(cuts))
        return jnp.repeat(jnp.exp(draws), dims[dim] // shards_of).reshape((-1,) + (1,) * (len(dims) - dim - 1))

    loudness = one(*cuts[0])
    for cut in cuts[1:]:
        loudness = loudness * one(*cut)
    return loudness


def normal_values(stream_key, extent, deviation, bound, cuts=(), kind=jnp.bfloat16):
    loudness = block_scale(stream_key, extent, cuts, -0.22, 0.18) if cuts else 1.0
    entries = jax.random.normal(stream_key, extent, jnp.float32) * deviation * loudness
    return jnp.minimum(jnp.maximum(entries, -bound), bound).astype(kind)


def setup_inputs(seed: int = 0) -> dict:
    splits = jax.random.split(jax.random.key(seed), 11)
    final_adjoint = normal_values(splits[0], (FIELDS, MODES, ELEMS), 1.0, 6.0, ((2, 512),), jnp.float32)
    star_mats = draw_star_mats(jax.random.fold_in(splits[10], 71), 0)
    deriv_stiff = draw_deriv_stiff(jax.random.fold_in(splits[10], 71), 0)
    volume_stiffness = normal_values(splits[3], (3, MODES, MODES), 0.035, 0.21875, (), jnp.float32)
    face_projection = normal_values(splits[4], (4, FACE_MODES, MODES), MODES ** -0.5, 0.75, (), jnp.float32)
    flux_local = normal_values(splits[5], (4, FIELDS, FIELDS, ELEMS), 0.15, 0.875, ((3, 512),), jnp.float32)
    flux_across = normal_values(splits[6], (4, FIELDS, FIELDS, ELEMS), 0.15, 0.875, ((3, 512),), jnp.float32)
    cluster = draw_cluster(jax.random.fold_in(splits[10], 71), 0)
    partner = draw_partner(jax.random.fold_in(splits[10], 71), 0)
    send_slots = draw_send_slots(jax.random.fold_in(splits[10], 71), 0)
    return {"final_adjoint": final_adjoint, "star_mats": star_mats, "deriv_stiff": deriv_stiff, "volume_stiffness": volume_stiffness, "face_projection": face_projection, "flux_local": flux_local, "flux_across": flux_across, "cluster": cluster, "partner": partner, "send_slots": send_slots}


HIGH_ORDER = lax.Precision.HIGHEST


def coefficients(lower, upper):
    return [(upper ** (k + 1) - lower ** (k + 1)) / math.factorial(k + 1) for k in range(TERMS)]


def derive_terms(value_rows, stiff, matrix_list):
    turned = jnp.einsum("dmn,fme->dfne", stiff, value_rows, precision=HIGH_ORDER)
    return jnp.einsum("dgfe,dfne->gne", matrix_list, turned, precision=HIGH_ORDER)


def face_terms(adjoint, face_projection, flux_local, flux_across):
    traces = jnp.einsum("cbm,fme->fbce", face_projection, adjoint, precision=HIGH_ORDER)
    own_element = jnp.einsum("cgfe,fbce->gbce", flux_local, traces, precision=HIGH_ORDER)
    sent = jnp.einsum("cgfe,fbce->gbce", flux_across, traces, precision=HIGH_ORDER)
    return own_element, sent


def blocks(array, groups):
    leading = array.shape[:-1]
    split = array.reshape(leading + (groups, -1))
    return jnp.moveaxis(split, -2, 0)


def unblocks(array):
    joined = jnp.moveaxis(array, 0, -2)
    return joined.reshape(joined.shape[:-2] + (-1,))


def from_lower(value_rows, axis):
    widths = [(0, 0)] * value_rows.ndim
    widths[axis] = (1, 0)
    return lax.slice_in_dim(jnp.pad(value_rows, widths), 0, value_rows.shape[axis], axis=axis)


def from_upper(value_rows, axis):
    widths = [(0, 0)] * value_rows.ndim
    widths[axis] = (0, 1)
    return lax.slice_in_dim(jnp.pad(value_rows, widths), 1, value_rows.shape[axis] + 1, axis=axis)


def neighbours(boxes):
    grid = boxes.reshape((N_GX, N_GY, N_GZ) + boxes.shape[1:])
    pieces = [from_lower(grid[..., 1, :], 0), from_upper(grid[..., 0, :], 0),
              from_lower(grid[..., 3, :], 1), from_upper(grid[..., 2, :], 1),
              from_lower(grid[..., 5, :], 2), from_upper(grid[..., 4, :], 2)]
    stacked = jnp.stack(pieces, axis=-2)
    return stacked.reshape((boxes.shape[0], boxes.shape[1], -1))


def horner_rows(source_field, rows, stiff, matrix_list):
    total = rows[TERMS - 1] * source_field
    for k in range(TERMS - 2, -1, -1):
        total = rows[k] * source_field + derive_terms(total, stiff, matrix_list)
    return total


def reference(final_adjoint, star_mats, deriv_stiff, volume_stiffness, face_projection, flux_local, flux_across, cluster, partner, send_slots):
    groups = N_GX * N_GY * N_GZ
    fine = 1.0 / FINE_STEPS
    adjoint = blocks(final_adjoint, groups)
    mats_all = blocks(star_mats, groups)
    local_all = blocks(flux_local, groups)
    across_all = blocks(flux_across, groups)
    kinds_all = blocks(cluster, groups)
    links_all = blocks(partner, groups)
    lists_all = blocks(send_slots, groups)
    store = jnp.zeros_like(adjoint)
    fast_rows = coefficients(0.0, fine)
    for step in range(FINE_STEPS - 1, -1, -1):
        slow_rows = coefficients(step * fine, (step + 1) * fine)

        def outgoing(entry):
            value_rows, local_mats, across_mats, listing = entry
            own_element, sent = face_terms(value_rows, face_projection, local_mats, across_mats)
            sent_flat = sent.reshape(sent.shape[0] * sent.shape[1], -1)
            return jnp.take(sent_flat, listing, axis=1)

        boxes = lax.map(outgoing, (adjoint, local_all, across_all, lists_all))
        received = neighbours(boxes)

        def advance(entry):
            value_rows, matrix_list, local_mats, across_mats, kinds, links, arrived, kept = entry
            own_element, sent = face_terms(value_rows, face_projection, local_mats, across_mats)
            sent_flat = sent.reshape(sent.shape[0] * sent.shape[1], -1)
            extended = jnp.concatenate([sent_flat, arrived], axis=1)
            incoming_flux = jnp.take(extended, links.reshape(-1).astype(jnp.int32), axis=1).reshape(own_element.shape)
            source_field = derive_terms(value_rows, volume_stiffness, matrix_list) + jnp.einsum("mpu,apmx->aux", face_projection, own_element + incoming_flux, precision=HIGH_ORDER)
            rows = [jnp.where(kinds == 0, fast_rows[k], slow_rows[k]) for k in range(TERMS)]
            change = horner_rows(source_field, rows, deriv_stiff, matrix_list)
            fast_share = (kinds == 0).astype(jnp.float32)
            return value_rows + change * fast_share, kept + change * (1.0 - fast_share)

        adjoint, store = lax.map(advance, (adjoint, mats_all, local_all, across_all, kinds_all, links_all, received, store))
    return unblocks(adjoint + store)
```

```python
import math

import jax
import jax.numpy as jnp
from jax import lax
from jax.experimental import pallas as pl
from jax.experimental.pallas import tpu as pltpu
from jax.sharding import PartitionSpec as P

MESH = pl.DeviceIdType.MESH
TERMS = 6
STEPS = 4
FINE = 1.0 / STEPS
NF = 9
NM = 56
NB = 21
PB = 24
LN = 128
F32 = jnp.float32
B16 = jnp.bfloat16


def coefficients(lower, upper):
    return [(upper ** (k + 1) - lower ** (k + 1)) / math.factorial(k + 1) for k in range(TERMS)]


FAST = coefficients(0.0, FINE)
WHOLE = coefficients(0.0, 1.0)
SLOW = [coefficients(s * FINE, (s + 1) * FINE) for s in range(STEPS)]


def two(x):
    high = x.astype(B16)
    return high, (x - high.astype(F32)).astype(B16)


def nn(a, b):
    return jnp.dot(a, b, preferred_element_type=F32)


def nt(a, b):
    return lax.dot_general(a, b, (((1,), (1,)), ((), ())), preferred_element_type=F32)


def stack3(x):
    high, low = two(x)
    return jnp.concatenate([high, low, high], axis=0)


def left3(x):
    high, low = two(x)
    return jnp.concatenate([high, high, low], axis=1)


def rows64(x):
    return jnp.concatenate([x, jnp.zeros((64 - NM, LN), F32)], axis=0)


def iota(shape, dim):
    return lax.broadcasted_iota(jnp.int32, shape, dim).astype(F32)


def hot(mask):
    return jnp.where(mask, 1.0, 0.0)


def pick(a, cm2):
    high, low = two(a)
    return nt(high, cm2) + nt(low, cm2)


def kernel(
    y_ref, star_ref, ds_ref, vs_ref, fp_ref, fl_ref, fa_ref, cl_ref, pa_ref, ss_ref, o_ref,
    A3, V3, P3, PT3, PF, AF, X9, Xp, T9, Tp, TR9, TRp, SF, SS, CE, CO, STARF, FLF, FAF, Yp, Sp, SB, MF, Z9, Zp, TOT,
    send3, recv3, send, recv, ssem3, rsem3, ssem, rsem,
):
    place = [lax.axis_index(a) for a in ("gx", "gy", "gz")]
    sizes = [lax.axis_size(a) for a in ("gx", "gy", "gz")]
    sides = []
    for d in range(6):
        axis, up = d // 2, d % 2
        there = place[axis] < sizes[axis] - 1 if up else place[axis] > 0
        target = list(place)
        target[axis] = place[axis] + (1 if up else -1)
        sides.append((there, tuple(target)))
    peers = sum(there.astype(jnp.int32) for there, _ in sides)

    barrier = pltpu.get_barrier_semaphore()
    for there, target in sides:
        @pl.when(there)
        def _():
            pl.semaphore_signal(barrier, inc=1, device_id=target, device_id_type=MESH)

    def link(s, d, arriving):
        to = d if arriving else d ^ 1
        target = sides[d][1]
        if s == STEPS - 1:
            pairs = [(send3.at[h, d], recv3.at[h, to], ssem3.at[h, d], rsem3.at[h, to]) for h in range(2)]
        else:
            pairs = [(send.at[s, d], recv.at[s, to], ssem.at[s, d], rsem.at[s, to])]
        return [
            pltpu.make_async_remote_copy(
                src_ref=a, dst_ref=b, send_sem=c, recv_sem=e, device_id=target, device_id_type=MESH)
            for a, b, c, e in pairs
        ]

    def start_all(s):
        for d in range(6):
            @pl.when(sides[d][0])
            def _():
                for copy in link(s, d, False):
                    copy.start()

    def arrive_all(s):
        for d in range(6):
            @pl.when(sides[d][0])
            def _():
                for copy in link(s, d, True):
                    copy.wait_recv()

    def sent_all(s):
        for d in range(6):
            @pl.when(sides[d][0])
            def _():
                for copy in link(s, d, False):
                    copy.wait_send()

    low_half = lax.broadcasted_iota(jnp.int32, (1, LN), 1) < 64

    PF[...] = jnp.zeros((96, LN), F32)
    for c in range(4):
        PF[c * PB : c * PB + NB, 0:NM] = fp_ref[c]
    pf = PF[...]
    P3[...] = left3(pf[:, 0:64])
    SF[...] = jnp.zeros(SF.shape, F32)
    for d in range(6):
        there, _ = sides[d]

        @pl.when(jnp.logical_not(there))
        def _():
            for half in range(2):
                recv3[half, d] = jnp.zeros((16, 256), F32)
            for s in range(STEPS - 1):
                recv[s, d] = jnp.zeros((16, 256), F32)

    for f in range(NF):
        X9[:, f * LN : (f + 1) * LN] = stack3(rows64(y_ref[f]))
    TR9[...] = nn(P3[...], X9[...])

    def flux_full(ref, emit):
        for c in range(4):
            acc = [None] * NF
            for f in range(NF):
                t = TR9[c * PB : (c + 1) * PB, f * LN : (f + 1) * LN]
                for g in range(NF):
                    p = ref[c, g, f : f + 1, :] * t
                    acc[g] = p if acc[g] is None else acc[g] + p
            for g in range(NF):
                emit(c, g, acc[g])

    def put_sent(c, g, value):
        SF[g * PB : (g + 1) * PB, c * LN : (c + 1) * LN] = value

    flux_full(fa_ref, put_sent)

    fast = hot(cl_ref[...] == 0)
    fast512 = jnp.concatenate([fast] * 4, axis=1)
    slow512 = 1.0 - fast512
    eye = iota((32, 32), 0) == iota((32, 32), 1)
    lane512 = iota((32, 512), 1)
    parts = []
    for d in range(6):
        row = ss_ref[d : d + 1, :].astype(F32)
        column = jnp.sum(jnp.where(eye, row, 0.0), axis=1, keepdims=True)
        parts.append(hot(lane512 == column))
    slots = jnp.concatenate(parts, axis=0).astype(B16)
    flags = nt(jnp.broadcast_to(fast512, (16, 512)).astype(B16), slots)
    i_sub, i_lane = lax.broadcasted_iota(jnp.int32, (192, 192), 0), lax.broadcasted_iota(jnp.int32, (192, 192), 1)
    earlier = hot(jnp.logical_and(i_sub // 32 == i_lane // 32, i_sub < i_lane)).astype(B16)
    ranks = nn(flags.astype(B16), earlier)[0:1, :]
    flags = flags[0:1, :]
    lane192 = lax.broadcasted_iota(jnp.int32, (1, 192), 1)
    j_row = (lane192 % 32).astype(F32)
    position = jnp.where(flags > 0.5, ranks, 31.0 - (j_row - ranks))
    row_of = (lane192 // 32).astype(F32) * 16.0 + position + jnp.where(position > 15.5, 80.0, 0.0)
    moved = hot(i_sub.astype(F32) == row_of)
    j_column = jnp.sum(moved * j_row, axis=1, keepdims=True)
    fast_column = jnp.sum(moved * flags, axis=1, keepdims=True)
    ordered = nn(moved.astype(B16), slots).astype(B16)

    sent_hi, sent_lo = two(SF[...])
    out3 = nt(ordered, sent_hi) + nt(ordered, sent_lo)
    out3 = out3 + jnp.where(lax.broadcasted_iota(jnp.int32, (192, 256), 1) == 216, j_column, 0.0)
    for half in range(2):
        for d in range(6):
            r = half * 96 + d * 16
            send3[half, d] = out3[r : r + 16, :]
    send_constant = out3[0:96, :] * (1.0 - fast_column[0:96, :])

    pl.semaphore_wait(barrier, peers)
    start_all(STEPS - 1)

    AF[...] = jnp.zeros(AF.shape, F32)
    for d in range(3):
        AF[d * NM : (d + 1) * NM, 0:NM] = jnp.transpose(ds_ref[d])
    A3[...] = left3(AF[:, 0:64])
    for d in range(3):
        AF[d * NM : (d + 1) * NM, 0:NM] = jnp.transpose(vs_ref[d])
    V3[...] = left3(AF[:, 0:64])
    PT3[...] = left3(jnp.transpose(pf)[0:64, :])

    before = hot(iota((LN, LN), 0) < iota((LN, LN), 1)).astype(B16)
    rank = nn(jnp.broadcast_to(fast, (16, LN)).astype(B16), before)[0:1, :]
    sub = iota((LN, LN), 0)
    cm2 = jnp.concatenate([hot(sub == rank) * fast, hot(sub == rank + 64.0) * fast], axis=1).astype(B16)

    def compact_mats(ref, lead, out):
        CE[...] = jnp.zeros(CE.shape, F32)
        CO[...] = jnp.zeros(CO.shape, F32)
        for d in range(lead):
            for g in range(NF):
                r = (d * NF + g) * 8
                CE[r : r + 5, :] = ref[d, g, 0:5, :]
                CO[r : r + 4, :] = ref[d, g, 5:9, :]
        if lead == 3:
            for g in range(NF):
                CO[g * 8 + 4 : g * 8 + 5, :] = ref[1, g, 4:5, :]
        n = lead * NF * 8
        out[...] = pick(jnp.concatenate([CE[0:n, :], CO[0:n, :]], axis=1), cm2)

    compact_mats(star_ref, 3, STARF)
    compact_mats(fl_ref, 4, FLF)
    compact_mats(fa_ref, 4, FAF)

    def second(k):
        return k + 5 if k < 4 else 4

    for k in range(5):
        Yp[:, k * LN : (k + 1) * LN] = pick(jnp.concatenate([y_ref[k], y_ref[second(k)]], axis=1), cm2)

    partner = jnp.concatenate([pa_ref[c : c + 1, :] for c in range(4)], axis=1).astype(F32)
    local = hot(iota((512, 512), 0) == partner).astype(B16)
    local_fast = jnp.concatenate(
        [nn(cm2, local[0:256, :]), nn(cm2, local[256:512, :])], axis=0
    ).astype(B16)

    def to_fast(a):
        return jnp.concatenate([nt(a[:, 0:256], cm2), nt(a[:, 256:512], cm2)], axis=1).astype(B16)

    local_ff = to_fast(local_fast)
    local_fs = (local_fast.astype(F32) * slow512).astype(B16)
    ordered_fast = to_fast(ordered[0:96, :])

    slow_hi = (sent_hi.astype(F32) * slow512).astype(B16)[0:224, :]
    slow_lo = (sent_lo.astype(F32) * slow512).astype(B16)[0:224, :]
    constant = nn(slow_hi, local) + nn(slow_lo, local)
    for i in range(2):
        cols = slice(i * 256, (i + 1) * 256)
        SS[:, i * LN : (i + 1) * LN] = nt(sent_hi[:, cols], cm2) + nt(sent_lo[:, cols], cm2)

    def put_own(c, g, value):
        Z9[c * PB : (c + 1) * PB, g * LN : (g + 1) * LN] = value

    flux_full(fl_ref, put_own)

    def star_full(emit):
        for base in (0, 3, 6):
            acc = [None] * 3
            for d in range(3):
                for f in range(NF):
                    t = T9[d * NM : (d + 1) * NM, f * LN : (f + 1) * LN]
                    for q in range(3):
                        p = star_ref[d, base + q, f : f + 1, :] * t
                        acc[q] = p if acc[q] is None else acc[q] + p
            for q in range(3):
                emit(base + q, acc[q])

    T9[...] = nn(V3[...], X9[...])

    def put_base(g, value):
        SB[:, g * LN : (g + 1) * LN] = value

    star_full(put_base)

    arrive_all(STEPS - 1)
    first = jnp.concatenate([recv3[half, d] for half in range(2) for d in range(6)], axis=0)
    row192 = lax.broadcasted_iota(jnp.int32, (192, 1), 0)
    side = (row192 % 96) // 16
    remote = hot(partner == 512.0 + side.astype(F32) * 32.0 + first[:, 216:217]).astype(B16)
    remote_ff = to_fast(remote[0:96, :])
    remote_fs = (remote[0:96, :].astype(F32) * slow512).astype(B16)

    def turned(a):
        return two(jnp.transpose(a)[0:224, :])

    late_hi, late_lo = turned(first[96:192, :])
    constant = constant + nn(late_hi, remote[96:192, :]) + nn(late_lo, remote[96:192, :])
    for c in range(4):
        for g in range(NF):
            Z9[c * PB : (c + 1) * PB, g * LN : (g + 1) * LN] += constant[g * PB : (g + 1) * PB, c * LN : (c + 1) * LN]
    constant_fast = pick_two(constant, cm2)
    SB[...] += nn(PT3[...], stack3(Z9[...]))[0:NM, :]
    for k in range(5):
        Sp[:, k * LN : (k + 1) * LN] = pick(
            jnp.concatenate([SB[:, k * LN : (k + 1) * LN], SB[:, second(k) * LN : (second(k) + 1) * LN]], axis=1), cm2
        )
    slow128 = 1.0 - fast
    for g in range(NF):
        SB[:, g * LN : (g + 1) * LN] = SB[:, g * LN : (g + 1) * LN] * slow128

    def star_fast(emit):
        t01 = jnp.where(low_half, Tp[0:NM, 512:640], Tp[NM : 2 * NM, 512:640])
        for block in ((0, 5, 1, 6), (2, 7, 3, 8), (4,)):
            acc = [star_base(t01, g) + STARF[(18 + g) * 8 + 4 : (18 + g) * 8 + 5, :] * Tp[2 * NM : 3 * NM, 512:640] for g in block]
            for d in range(3):
                for k in range(4):
                    t = Tp[d * NM : (d + 1) * NM, k * LN : (k + 1) * LN]
                    for q, g in enumerate(block):
                        r = (d * NF + g) * 8 + k
                        acc[q] = acc[q] + STARF[r : r + 1, :] * t
            if len(block) == 1:
                emit(4, acc[0] + pltpu.roll(acc[0], 64, 1))
            else:
                for q in (0, 2):
                    emit(block[q], halves(acc[q], acc[q + 1]))

    def star_base(t01, g):
        return STARF[g * 8 + 4 : g * 8 + 5, :] * t01

    def halves(a, b):
        return jnp.where(low_half, a, b) + pltpu.roll(jnp.where(low_half, b, a), 64, 1)

    def flux_fast(ref, c):
        acc = [None] * NF
        for k in range(5):
            t = TRp[c * PB : (c + 1) * PB, k * LN : (k + 1) * LN]
            for g in range(NF):
                r = (c * NF + g) * 8 + k
                p = ref[r : r + 1, :] * t
                acc[g] = p if acc[g] is None else acc[g] + p
        return acc

    def put_x(k, value):
        Xp[:, k * LN : (k + 1) * LN] = stack3(rows64(value))

    def arrange(a, add):
        for k in range(5):
            for i in range(2):
                e = a[k * PB : (k + 1) * PB, i * LN : (i + 1) * LN]
                o = a[second(k) * PB : (second(k) + 1) * PB, i * LN : (i + 1) * LN]
                c = 2 * i
                v0 = jnp.where(low_half, e, pltpu.roll(o, 64, 1))
                v1 = jnp.where(low_half, pltpu.roll(e, 64, 1), o)
                cols = slice(k * LN, (k + 1) * LN)
                if add:
                    Zp[c * PB : (c + 1) * PB, cols] += v0
                    Zp[(c + 1) * PB : (c + 2) * PB, cols] += v1
                else:
                    Zp[c * PB : (c + 1) * PB, cols] = v0
                    Zp[(c + 1) * PB : (c + 2) * PB, cols] = v1

    def horner_fast():
        for k in range(5):
            put_x(k, FAST[TERMS - 1] * Sp[:, k * LN : (k + 1) * LN])

        def level(i, c):
            Tp[...] = nn(A3[...], Xp[...])

            def emit(k, value):
                total = value + c * Sp[:, k * LN : (k + 1) * LN]
                TOT[:, k * LN : (k + 1) * LN] = total
                put_x(k, total)

            star_fast(emit)
            return c * ((TERMS - 1 - i).astype(F32) * (1.0 / FINE))

        lax.fori_loop(0, TERMS - 1, level, jnp.float32(FAST[TERMS - 2]))
        for k in range(5):
            cols = slice(k * LN, (k + 1) * LN)
            value = Yp[:, cols] + TOT[:, cols]
            Yp[:, cols] = value
            put_x(k, value)

    def slow_source(s, hi, lo, r_hi, r_lo):
        got = nn(hi, local_fs) + nn(lo, local_fs) + nn(r_hi, remote_fs) + nn(r_lo, remote_fs)
        for c in range(4):
            for g in range(NF):
                Z9[c * PB : (c + 1) * PB, g * LN : (g + 1) * LN] = got[g * PB : (g + 1) * PB, c * LN : (c + 1) * LN]
        MF[s] = nn(PT3[...], stack3(Z9[...]))[0:NM, :]

    def fast_gather(hi, lo, r_hi, r_lo):
        return nn(hi, local_ff) + nn(lo, local_ff) + nn(r_hi, remote_ff) + nn(r_lo, remote_ff)

    hi, lo = two(SS[...])
    hi, lo = hi[0:224, :], lo[0:224, :]
    r_hi, r_lo = turned(first[0:96, :])
    arrange(fast_gather(hi, lo, r_hi, r_lo), False)
    Sp[...] += nn(PT3[...], stack3(Zp[...]))[0:NM, :]
    slow_source(STEPS - 1, hi, lo, r_hi, r_lo)
    horner_fast()

    for s in range(STEPS - 2, -1, -1):
        TRp[...] = nn(P3[...], Xp[...])
        for i in range(2):
            a0, a1 = flux_fast(FAF, 2 * i), flux_fast(FAF, 2 * i + 1)
            for g in range(NF):
                SS[g * PB : (g + 1) * PB, i * LN : (i + 1) * LN] = halves(a0[g], a1[g])
        hi, lo = two(SS[...])
        out = nt(ordered_fast, hi) + nt(ordered_fast, lo) + send_constant
        for d in range(6):
            send[s, d] = out[d * 16 : (d + 1) * 16, :]
        start_all(s)

        Tp[...] = nn(V3[...], Xp[...])

        def put_source(k, value):
            Sp[:, k * LN : (k + 1) * LN] = value

        star_fast(put_source)
        for c in range(4):
            acc = flux_fast(FLF, c)
            for k in range(5):
                value = halves(acc[k], acc[k + 5]) if k < 4 else acc[4] + pltpu.roll(acc[4], 64, 1)
                Zp[c * PB : (c + 1) * PB, k * LN : (k + 1) * LN] = value
        hi, lo = hi[0:224, :], lo[0:224, :]

        arrive_all(s)
        r_hi, r_lo = turned(jnp.concatenate([recv[s, d] for d in range(6)], axis=0))
        arrange(fast_gather(hi, lo, r_hi, r_lo) + constant_fast, True)
        Sp[...] += nn(PT3[...], stack3(Zp[...]))[0:NM, :]
        slow_source(s, hi, lo, r_hi, r_lo)
        if s > 0:
            horner_fast()

    spread = cm2
    s_hi, s_lo = two(Sp[...])
    y_hi, y_lo = two(Yp[...])
    for k in range(5):
        cols = slice(k * LN, (k + 1) * LN)
        source = nn(s_hi[:, cols], spread) + nn(s_lo[:, cols], spread)
        value = nn(y_hi[:, cols], spread) + nn(y_lo[:, cols], spread)
        for q, f in enumerate((k, k + 5) if k < 4 else (4,)):
            MF[0, :, f * LN : (f + 1) * LN] += source[:, q * LN : (q + 1) * LN]
            TOT9 = value[:, q * LN : (q + 1) * LN] + y_ref[f] * slow128
            o_ref[f] = TOT9

    def weighted(k, g):
        cols = slice(g * LN, (g + 1) * LN)
        total = WHOLE[k] * SB[:, cols]
        for s in range(STEPS):
            total = total + SLOW[s][k] * MF[s, :, cols]
        return total

    for g in range(NF):
        X9[:, g * LN : (g + 1) * LN] = stack3(rows64(weighted(TERMS - 1, g)))
    for k in range(TERMS - 2, -1, -1):
        T9[...] = nn(A3[...], X9[...])

        def emit(g, value):
            total = value + weighted(k, g)
            if k > 0:
                X9[:, g * LN : (g + 1) * LN] = stack3(rows64(total))
            else:
                o_ref[g] += total

        star_full(emit)

    for s in range(STEPS):
        sent_all(s)


def pick_two(a, cm2):
    return jnp.concatenate([pick(a[:, 0:256], cm2), pick(a[:, 256:512], cm2)], axis=1)


def body(
    final_adjoint, star_mats, deriv_stiff, volume_stiffness, face_projection,
    flux_local, flux_across, cluster, partner, send_slots,
):
    V = pltpu.VMEM
    D = pltpu.SemaphoreType.DMA
    scratch = [
        V((168, 192), B16), V((168, 192), B16), V((96, 192), B16), V((64, 288), B16), V((96, LN), F32), V((168, LN), F32),
        V((192, 1152), B16), V((192, 640), B16), V((168, 1152), F32), V((168, 640), F32), V((96, 1152), F32), V((96, 640), F32),
        V((256, 512), F32), V((256, 256), F32), V((288, LN), F32), V((288, LN), F32),
        V((216, LN), F32), V((288, LN), F32), V((288, LN), F32),
        V((NM, 640), F32), V((NM, 640), F32), V((NM, 1152), F32), V((STEPS, NM, 1152), F32),
        V((96, 1152), F32), V((96, 640), F32), V((NM, 640), F32),
        V((2, 6, 16, 256), F32), V((2, 6, 16, 256), F32),
        V((STEPS - 1, 6, 16, 256), F32), V((STEPS - 1, 6, 16, 256), F32),
        D((2, 6)), D((2, 6)), D((STEPS - 1, 6)), D((STEPS - 1, 6)),
    ]
    return pl.pallas_call(
        kernel,
        out_shape=jax.ShapeDtypeStruct(final_adjoint.shape, F32),
        in_specs=[pl.BlockSpec(memory_space=pltpu.VMEM)] * 10,
        out_specs=pl.BlockSpec(memory_space=pltpu.VMEM),
        scratch_shapes=scratch,
        compiler_params=pltpu.CompilerParams(collective_id=0, has_side_effects=True, vmem_limit_bytes=48 * 2**20),
        name="coarse_step",
    )(
        final_adjoint, star_mats, deriv_stiff, volume_stiffness, face_projection,
        flux_local, flux_across, cluster.reshape(1, LN), partner, send_slots,
    )


def solution(mesh):
    every = ("gx", "gy", "gz")
    in_specs = (
        P(None, None, every), P(None, None, None, every), P(), P(), P(),
        P(None, None, None, every), P(None, None, None, every), P(every), P(None, every), P(None, every),
    )
    return jax.shard_map(body, mesh=mesh, in_specs=in_specs, out_specs=P(None, None, every), check_vma=False)
```

```python
import math

import jax
import jax.numpy as jnp
from jax import lax
from jax.experimental import pallas as pl
from jax.experimental.pallas import tpu as pltpu
from jax.sharding import PartitionSpec as P

MESH = pl.DeviceIdType.MESH
TERMS = 6
STEPS = 4
FINE = 1.0 / STEPS
NF = 9
NM = 56
NB = 21
PB = 24
LN = 128
F32 = jnp.float32
B16 = jnp.bfloat16


def coefficients(lower, upper):
    return [(upper ** (k + 1) - lower ** (k + 1)) / math.factorial(k + 1) for k in range(TERMS)]


FAST = coefficients(0.0, FINE)
WHOLE = coefficients(0.0, 1.0)
SLOW = [coefficients(s * FINE, (s + 1) * FINE) for s in range(STEPS)]


def two(x):
    high = x.astype(B16)
    return high, (x - high.astype(F32)).astype(B16)


def nn(a, b):
    return jnp.dot(a, b, preferred_element_type=F32)


def nt(a, b):
    return lax.dot_general(a, b, (((1,), (1,)), ((), ())), preferred_element_type=F32)


def stack3(x):
    high, low = two(x)
    return jnp.concatenate([high, low, high], axis=0)


def left3(x):
    high, low = two(x)
    return jnp.concatenate([high, high, low], axis=1)


def rows64(x):
    return jnp.concatenate([x, jnp.zeros((64 - NM, LN), F32)], axis=0)


def iota(shape, dim):
    return lax.broadcasted_iota(jnp.int32, shape, dim).astype(F32)


def hot(mask):
    return jnp.where(mask, 1.0, 0.0)


def pick(a, cm2):
    high, low = two(a)
    return nt(high, cm2) + nt(low, cm2)


def kernel(
    y_in, star_in, ds_in, vs_in, fp_in, fl_in, fa_in, cl_in, pa_in, ss_in, o_ref,
    y_ref, star_ref, ds_ref, vs_ref, fp_ref, fl_ref, fa_ref, cl_ref, pa_ref, ss_ref, insem,
    A3, V3, P3, PT3, PF, AF, X9, Xp, T9, Tp, TR9, TRp, SF, SS, CE, CO, STARF, FLF, FAF, Yp, Sp, SB, MF, Z9, Zp, TOT,
    send3, recv3, send, recv, ssem3, rsem3, ssem, rsem,
):
    loads = [
        pltpu.make_async_copy(a, b, insem.at[i])
        for i, (a, b) in enumerate((
            (fp_in, fp_ref), (y_in, y_ref), (fa_in, fa_ref), (cl_in, cl_ref), (ss_in, ss_ref),
            (ds_in, ds_ref), (vs_in, vs_ref), (pa_in, pa_ref), (star_in, star_ref), (fl_in, fl_ref),
        ))
    ]
    for load in loads:
        load.start()
    place = [lax.axis_index(a) for a in ("gx", "gy", "gz")]
    sizes = [lax.axis_size(a) for a in ("gx", "gy", "gz")]
    sides = []
    for d in range(6):
        axis, up = d // 2, d % 2
        there = place[axis] < sizes[axis] - 1 if up else place[axis] > 0
        target = list(place)
        target[axis] = place[axis] + (1 if up else -1)
        sides.append((there, tuple(target)))
    peers = sum(there.astype(jnp.int32) for there, _ in sides)

    barrier = pltpu.get_barrier_semaphore()
    for there, target in sides:
        @pl.when(there)
        def _():
            pl.semaphore_signal(barrier, inc=1, device_id=target, device_id_type=MESH)

    def link(s, d, arriving):
        to = d if arriving else d ^ 1
        target = sides[d][1]
        if s == STEPS - 1:
            pairs = [(send3.at[h, d], recv3.at[h, to], ssem3.at[h, d], rsem3.at[h, to]) for h in range(2)]
        else:
            pairs = [(send.at[s, d], recv.at[s, to], ssem.at[s, d], rsem.at[s, to])]
        return [
            pltpu.make_async_remote_copy(
                src_ref=a, dst_ref=b, send_sem=c, recv_sem=e, device_id=target, device_id_type=MESH)
            for a, b, c, e in pairs
        ]

    def start_all(s):
        for d in (5, 4, 1, 0, 3, 2):
            @pl.when(sides[d][0])
            def _():
                for copy in link(s, d, False):
                    copy.start()

    def arrive_all(s, which=range(6)):
        for d in which:
            @pl.when(sides[d][0])
            def _():
                for copy in link(s, d, True):
                    copy.wait_recv()

    def sent_all(s):
        for d in range(6):
            @pl.when(sides[d][0])
            def _():
                for copy in link(s, d, False):
                    copy.wait_send()

    low_half = lax.broadcasted_iota(jnp.int32, (1, LN), 1) < 64

    for load in loads[0:5]:
        load.wait()
    for b in range(NB):
        PF[b * 4 : b * 4 + 4, 0:NM] = fp_ref[b]
    pad = jnp.zeros((PB - NB, NM), F32)
    pf = jnp.concatenate(
        [r for c in range(4) for r in (PF[pl.ds(c, NB, stride=4), 0:NM], pad)], axis=0
    )
    pf = jnp.concatenate([pf, jnp.zeros((4 * PB, 64 - NM), F32)], axis=1)
    P3[...] = left3(pf)
    SF[NF * PB : 256, :] = jnp.zeros((256 - NF * PB, 512), F32)
    SS[NF * PB : 256, :] = jnp.zeros((256 - NF * PB, 256), F32)
    for f in range(NF):
        X9[:, f * LN : (f + 1) * LN] = stack3(rows64(y_ref[f]))
    TR9[...] = nn(P3[...], X9[...])

    def flux_full(ref, emit):
        for c in range(4):
            acc = [None] * NF
            for f in range(NF):
                t = TR9[c * PB : (c + 1) * PB, f * LN : (f + 1) * LN]
                for g in range(NF):
                    p = ref[g, f, c : c + 1, :] * t
                    acc[g] = p if acc[g] is None else acc[g] + p
            for g in range(NF):
                emit(c, g, acc[g])

    def put_sent(c, g, value):
        SF[g * PB : (g + 1) * PB, c * LN : (c + 1) * LN] = value

    flux_full(fa_ref, put_sent)

    fast = hot(cl_ref[...] == 0)
    fast512 = jnp.concatenate([fast] * 4, axis=1)
    slow512 = 1.0 - fast512
    eye = iota((32, 32), 0) == iota((32, 32), 1)
    lane512 = iota((32, 512), 1)
    parts = []
    for d in range(6):
        row = ss_ref[d : d + 1, :].astype(F32)
        column = jnp.sum(jnp.where(eye, row, 0.0), axis=1, keepdims=True)
        parts.append(hot(lane512 == column))
    slots = jnp.concatenate(parts, axis=0).astype(B16)
    flags = nt(jnp.broadcast_to(fast512, (16, 512)).astype(B16), slots)
    i_sub, i_lane = lax.broadcasted_iota(jnp.int32, (192, 192), 0), lax.broadcasted_iota(jnp.int32, (192, 192), 1)
    earlier = hot(jnp.logical_and(i_sub // 32 == i_lane // 32, i_sub < i_lane)).astype(B16)
    ranks = nn(flags.astype(B16), earlier)[0:1, :]
    flags = flags[0:1, :]
    lane192 = lax.broadcasted_iota(jnp.int32, (1, 192), 1)
    j_row = (lane192 % 32).astype(F32)
    position = jnp.where(flags > 0.5, ranks, 31.0 - (j_row - ranks))
    row_of = (lane192 // 32).astype(F32) * 16.0 + position + jnp.where(position > 15.5, 80.0, 0.0)
    moved = hot(i_sub.astype(F32) == row_of)
    j_column = jnp.sum(moved * j_row, axis=1, keepdims=True)
    fast_column = jnp.sum(moved * flags, axis=1, keepdims=True)
    ordered = nn(moved.astype(B16), slots).astype(B16)

    sent_hi, sent_lo = two(SF[...])
    out3 = nt(ordered, sent_hi) + nt(ordered, sent_lo)
    out3 = out3 + jnp.where(lax.broadcasted_iota(jnp.int32, (192, 256), 1) == 216, j_column, 0.0)
    for half in range(2):
        for d in range(6):
            r = half * 96 + d * 16
            send3[half, d] = out3[r : r + 16, :]
    send_constant = out3[0:96, :] * (1.0 - fast_column[0:96, :])

    pl.semaphore_wait(barrier, peers)
    start_all(STEPS - 1)

    for d in range(6):
        there, _ = sides[d]

        @pl.when(jnp.logical_not(there))
        def _():
            for half in range(2):
                recv3[half, d] = jnp.zeros((16, 256), F32)
            for s in range(STEPS - 1):
                recv[s, d] = jnp.zeros((16, 256), F32)

    for load in loads[5:]:
        load.wait()
    AF[...] = jnp.zeros(AF.shape, F32)
    for d in range(3):
        AF[d * NM : (d + 1) * NM, 0:NM] = jnp.transpose(ds_ref[d])
    A3[...] = left3(AF[:, 0:64])
    for d in range(3):
        AF[d * NM : (d + 1) * NM, 0:NM] = jnp.transpose(vs_ref[d])
    V3[...] = left3(AF[:, 0:64])
    PT3[...] = left3(jnp.transpose(pf))

    before = hot(iota((LN, LN), 0) < iota((LN, LN), 1)).astype(B16)
    rank = nn(jnp.broadcast_to(fast, (16, LN)).astype(B16), before)[0:1, :]
    sub = iota((LN, LN), 0)
    cm2 = jnp.concatenate([hot(sub == rank) * fast, hot(sub == rank + 64.0) * fast], axis=1).astype(B16)

    def compact_mats(ref, lead, out):
        CE[...] = jnp.zeros(CE.shape, F32)
        CO[...] = jnp.zeros(CO.shape, F32)
        for g in range(NF):
            for k in range(5):
                r = (g * 5 + k) * 4
                CE[r : r + lead, :] = ref[g, k]
                if k < 4:
                    CO[r : r + lead, :] = ref[g, k + 5]
                elif lead == 3:
                    CO[r : r + 1, :] = ref[g, 4, 1:2, :]
        out[...] = pick(jnp.concatenate([CE[...], CO[...]], axis=1), cm2)

    compact_mats(star_ref, 3, STARF)
    compact_mats(fl_ref, 4, FLF)
    compact_mats(fa_ref, 4, FAF)

    def second(k):
        return k + 5 if k < 4 else 4

    for k in range(5):
        Yp[:, k * LN : (k + 1) * LN] = pick(jnp.concatenate([y_ref[k], y_ref[second(k)]], axis=1), cm2)

    partner = jnp.concatenate([pa_ref[c : c + 1, :] for c in range(4)], axis=1).astype(F32)
    local = hot(iota((512, 512), 0) == partner).astype(B16)
    local_fast = jnp.concatenate(
        [nn(cm2, local[0:256, :]), nn(cm2, local[256:512, :])], axis=0
    ).astype(B16)

    def to_fast(a):
        return jnp.concatenate([nt(a[:, 0:256], cm2), nt(a[:, 256:512], cm2)], axis=1).astype(B16)

    local_ff = to_fast(local_fast)
    local_fs = (local_fast.astype(F32) * slow512).astype(B16)
    ordered_fast = to_fast(ordered[0:96, :])

    slow_hi = (sent_hi.astype(F32) * slow512).astype(B16)[0:224, :]
    slow_lo = (sent_lo.astype(F32) * slow512).astype(B16)[0:224, :]
    constant = nn(slow_hi, local) + nn(slow_lo, local)
    for i in range(2):
        cols = slice(i * 256, (i + 1) * 256)
        SS[:, i * LN : (i + 1) * LN] = nt(sent_hi[:, cols], cm2) + nt(sent_lo[:, cols], cm2)

    def put_own(c, g, value):
        Z9[c * PB : (c + 1) * PB, g * LN : (g + 1) * LN] = value

    flux_full(fl_ref, put_own)

    def star_full(emit):
        for base in (0, 3, 6):
            acc = [None] * 3
            for d in range(3):
                for f in range(NF):
                    t = T9[d * NM : (d + 1) * NM, f * LN : (f + 1) * LN]
                    for q in range(3):
                        p = star_ref[base + q, f, d : d + 1, :] * t
                        acc[q] = p if acc[q] is None else acc[q] + p
            for q in range(3):
                emit(base + q, acc[q])

    T9[...] = nn(V3[...], X9[...])

    def put_base(g, value):
        SB[:, g * LN : (g + 1) * LN] = value

    star_full(put_base)

    arrive_all(STEPS - 1)
    first = jnp.concatenate([recv3[half, d] for half in range(2) for d in range(6)], axis=0)
    row192 = lax.broadcasted_iota(jnp.int32, (192, 1), 0)
    side = (row192 % 96) // 16
    remote = hot(partner == 512.0 + side.astype(F32) * 32.0 + first[:, 216:217]).astype(B16)
    remote_ff = to_fast(remote[0:96, :])
    remote_fs = (remote[0:96, :].astype(F32) * slow512).astype(B16)

    def turned(a):
        return two(jnp.transpose(a)[0:224, :])

    late_hi, late_lo = turned(first[96:192, :])
    constant = constant + nn(late_hi, remote[96:192, :]) + nn(late_lo, remote[96:192, :])
    for c in range(4):
        for g in range(NF):
            Z9[c * PB : (c + 1) * PB, g * LN : (g + 1) * LN] += constant[g * PB : (g + 1) * PB, c * LN : (c + 1) * LN]
    constant_fast = pick_two(constant, cm2)
    SB[...] += nn(PT3[...], stack3(Z9[...]))[0:NM, :]
    for k in range(5):
        Sp[:, k * LN : (k + 1) * LN] = pick(
            jnp.concatenate([SB[:, k * LN : (k + 1) * LN], SB[:, second(k) * LN : (second(k) + 1) * LN]], axis=1), cm2
        )
    slow128 = 1.0 - fast
    for g in range(NF):
        SB[:, g * LN : (g + 1) * LN] = SB[:, g * LN : (g + 1) * LN] * slow128

    def star_fast(T, emit):
        for block in ((0, 5, 1, 6), (2, 7, 3, 8), (4,)):
            acc = [None] * len(block)

            def add(q, row, t):
                p = STARF[row : row + 1, :] * t
                acc[q] = p if acc[q] is None else acc[q] + p

            for k in range(4):
                for d in range(3):
                    t = T[d * NM : (d + 1) * NM, k * LN : (k + 1) * LN]
                    for q, g in enumerate(block):
                        add(q, (g * 5 + k) * 4 + d, t)
            last = slice(4 * LN, 5 * LN)
            t01 = jnp.where(low_half, T[0:NM, last], T[NM : 2 * NM, last])
            t2 = T[2 * NM : 3 * NM, last]
            for q, g in enumerate(block):
                add(q, (g * 5 + 4) * 4, t01)
                add(q, (g * 5 + 4) * 4 + 2, t2)
            if len(block) == 1:
                emit(4, acc[0] + pltpu.roll(acc[0], 64, 1))
            else:
                for q in (0, 2):
                    emit(block[q], halves(acc[q], acc[q + 1]))

    def halves(a, b):
        return jnp.where(low_half, a, b) + pltpu.roll(jnp.where(low_half, b, a), 64, 1)

    def flux_fast(ref, c):
        acc = [None] * NF
        for k in range(5):
            t = TRp[c * PB : (c + 1) * PB, k * LN : (k + 1) * LN]
            for g in range(NF):
                r = (g * 5 + k) * 4 + c
                p = ref[r : r + 1, :] * t
                acc[g] = p if acc[g] is None else acc[g] + p
        return acc

    def put_x(k, value):
        Xp[:, k * LN : (k + 1) * LN] = stack3(rows64(value))

    def arrange(a, add):
        for k in range(5):
            for i in range(2):
                e = a[k * PB : (k + 1) * PB, i * LN : (i + 1) * LN]
                o = a[second(k) * PB : (second(k) + 1) * PB, i * LN : (i + 1) * LN]
                c = 2 * i
                v0 = jnp.where(low_half, e, pltpu.roll(o, 64, 1))
                v1 = jnp.where(low_half, pltpu.roll(e, 64, 1), o)
                cols = slice(k * LN, (k + 1) * LN)
                if add:
                    Zp[c * PB : (c + 1) * PB, cols] += v0
                    Zp[(c + 1) * PB : (c + 2) * PB, cols] += v1
                else:
                    Zp[c * PB : (c + 1) * PB, cols] = v0
                    Zp[(c + 1) * PB : (c + 2) * PB, cols] = v1

    def horner_fast():
        for k in range(5):
            put_x(k, FAST[TERMS - 1] * Sp[:, k * LN : (k + 1) * LN])

        def level(i, c):
            Tp[...] = nn(A3[...], Xp[...])

            def emit(k, value):
                total = value + c * Sp[:, k * LN : (k + 1) * LN]
                TOT[:, k * LN : (k + 1) * LN] = total
                put_x(k, total)

            star_fast(Tp, emit)
            return c * ((TERMS - 1 - i).astype(F32) * (1.0 / FINE))

        lax.fori_loop(0, TERMS - 1, level, jnp.float32(FAST[TERMS - 2]))
        for k in range(5):
            cols = slice(k * LN, (k + 1) * LN)
            value = Yp[:, cols] + TOT[:, cols]
            Yp[:, cols] = value
            put_x(k, value)

    def gather(pairs):
        total = None
        for high, low, ones in pairs:
            got = nn(high, ones) + nn(low, ones)
            total = got if total is None else total + got
        return total

    def slow_source(s, got):
        for c in range(4):
            for g in range(NF):
                Z9[c * PB : (c + 1) * PB, g * LN : (g + 1) * LN] = got[g * PB : (g + 1) * PB, c * LN : (c + 1) * LN]
        MF[s] = nn(PT3[...], stack3(Z9[...]))[0:NM, :]

    def twice(pair):
        return jnp.concatenate(pair, axis=1)

    near_ff, far_ff = remote_ff[0:64, :], jnp.concatenate([remote_ff[64:96, :]] * 2, axis=0)
    near_fs, far_fs = remote_fs[0:64, :], jnp.concatenate([remote_fs[64:96, :]] * 2, axis=0)

    hi, lo = two(SS[...])
    hi, lo = hi[0:224, :], lo[0:224, :]
    r_hi, r_lo = turned(first[0:96, :])
    arrange(gather([(hi, lo, local_ff), (r_hi, r_lo, remote_ff)]), False)
    Sp[...] += nn(PT3[...], stack3(Zp[...]))[0:NM, :]
    horner_fast()
    waiting = [(hi, lo, local_fs), (r_hi, r_lo, remote_fs)]

    for s in range(STEPS - 2, -1, -1):
        TRp[...] = nn(P3[...], Xp[...])
        for i in range(2):
            a0, a1 = flux_fast(FAF, 2 * i), flux_fast(FAF, 2 * i + 1)
            for g in range(NF):
                SS[g * PB : (g + 1) * PB, i * LN : (i + 1) * LN] = halves(a0[g], a1[g])
        hi, lo = two(SS[...])
        out = nt(ordered_fast, hi) + nt(ordered_fast, lo) + send_constant
        for d in range(6):
            send[s, d] = out[d * 16 : (d + 1) * 16, :]
        start_all(s)

        hi, lo = hi[0:224, :], lo[0:224, :]
        Tp[...] = nn(V3[...], Xp[...])

        def put_source(k, value):
            Sp[:, k * LN : (k + 1) * LN] = value

        star_fast(Tp, put_source)
        for c in range(4):
            acc = flux_fast(FLF, c)
            for k in range(5):
                value = halves(acc[k], acc[k + 5]) if k < 4 else acc[4] + pltpu.roll(acc[4], 64, 1)
                Zp[c * PB : (c + 1) * PB, k * LN : (k + 1) * LN] = value
        slow_source(s + 1, gather(waiting))

        arrive_all(s, (0, 1, 2, 3))
        r_hi, r_lo = turned(jnp.concatenate([recv[s, d] for d in range(4)], axis=0))
        arrange(gather([(hi, lo, local_ff), (r_hi, r_lo, near_ff)]) + constant_fast, True)
        Sp[...] += nn(PT3[...], stack3(Zp[...]))[0:NM, :]
        waiting = [(hi, lo, local_fs), (r_hi, r_lo, near_fs)]
        if s == 0:
            slow_source(0, gather(waiting))

        arrive_all(s, (4, 5))
        far = twice(turned(jnp.concatenate([recv[s, d] for d in (4, 5)], axis=0)))
        arrange(nn(far, far_ff), False)
        Sp[...] += nn(PT3[...], stack3(Zp[...]))[0:NM, :]
        if s > 0:
            horner_fast()
            waiting.append((far[:, 0:32], far[:, 32:64], remote_fs[64:96, :]))
        else:
            got = nn(far, far_fs)
            for c in range(4):
                for g in range(NF):
                    Z9[c * PB : (c + 1) * PB, g * LN : (g + 1) * LN] = got[g * PB : (g + 1) * PB, c * LN : (c + 1) * LN]
            MF[0] += nn(PT3[...], stack3(Z9[...]))[0:NM, :]

    spread = cm2
    s_hi, s_lo = two(Sp[...])
    y_hi, y_lo = two(Yp[...])
    for k in range(5):
        cols = slice(k * LN, (k + 1) * LN)
        source = nn(s_hi[:, cols], spread) + nn(s_lo[:, cols], spread)
        value = nn(y_hi[:, cols], spread) + nn(y_lo[:, cols], spread)
        for q, f in enumerate((k, k + 5) if k < 4 else (4,)):
            MF[0, :, f * LN : (f + 1) * LN] += source[:, q * LN : (q + 1) * LN]
            TOT9 = value[:, q * LN : (q + 1) * LN] + y_ref[f] * slow128
            o_ref[f] = TOT9

    def weighted(k, g):
        cols = slice(g * LN, (g + 1) * LN)
        total = WHOLE[k] * SB[:, cols]
        for s in range(STEPS):
            total = total + SLOW[s][k] * MF[s, :, cols]
        return total

    for g in range(NF):
        X9[:, g * LN : (g + 1) * LN] = stack3(rows64(weighted(TERMS - 1, g)))
    for k in range(TERMS - 2, -1, -1):
        T9[...] = nn(A3[...], X9[...])

        def emit(g, value):
            total = value + weighted(k, g)
            if k > 0:
                X9[:, g * LN : (g + 1) * LN] = stack3(rows64(total))
            else:
                o_ref[g] += total

        star_full(emit)

    for s in range(STEPS):
        sent_all(s)


def pick_two(a, cm2):
    return jnp.concatenate([pick(a[:, 0:256], cm2), pick(a[:, 256:512], cm2)], axis=1)


def body(
    final_adjoint, star_mats, deriv_stiff, volume_stiffness, face_projection,
    flux_local, flux_across, cluster, partner, send_slots,
):
    V = pltpu.VMEM
    D = pltpu.SemaphoreType.DMA
    views = (
        final_adjoint, jnp.transpose(star_mats, (1, 2, 0, 3)), deriv_stiff, volume_stiffness,
        jnp.transpose(face_projection, (1, 0, 2)), jnp.transpose(flux_local, (1, 2, 0, 3)),
        jnp.transpose(flux_across, (1, 2, 0, 3)), cluster.reshape(1, LN), partner, send_slots,
    )
    scratch = [V(a.shape, a.dtype) for a in views] + [
        D((10,)),
        V((168, 192), B16), V((168, 192), B16), V((96, 192), B16), V((64, 288), B16), V((96, LN), F32), V((168, LN), F32),
        V((192, 1152), B16), V((192, 640), B16), V((168, 1152), F32), V((168, 640), F32), V((96, 1152), F32), V((96, 640), F32),
        V((256, 512), F32), V((256, 256), F32), V((184, LN), F32), V((184, LN), F32),
        V((184, LN), F32), V((184, LN), F32), V((184, LN), F32),
        V((NM, 640), F32), V((NM, 640), F32), V((NM, 1152), F32), V((STEPS, NM, 1152), F32),
        V((96, 1152), F32), V((96, 640), F32), V((NM, 640), F32),
        V((2, 6, 16, 256), F32), V((2, 6, 16, 256), F32),
        V((STEPS - 1, 6, 16, 256), F32), V((STEPS - 1, 6, 16, 256), F32),
        D((2, 6)), D((2, 6)), D((STEPS - 1, 6)), D((STEPS - 1, 6)),
    ]
    return pl.pallas_call(
        kernel,
        out_shape=jax.ShapeDtypeStruct(final_adjoint.shape, F32),
        in_specs=[pl.BlockSpec(memory_space=pltpu.HBM)] * 10,
        out_specs=pl.BlockSpec(memory_space=pltpu.VMEM),
        scratch_shapes=scratch,
        compiler_params=pltpu.CompilerParams(collective_id=0, has_side_effects=True, vmem_limit_bytes=64 * 2**20),
        name="coarse_step",
    )(*views)


def solution(mesh):
    every = ("gx", "gy", "gz")
    in_specs = (
        P(None, None, every), P(None, None, None, every), P(), P(), P(),
        P(None, None, None, every), P(None, None, None, every), P(every), P(None, every), P(None, every),
    )
    return jax.shard_map(body, mesh=mesh, in_specs=in_specs, out_specs=P(None, None, every), check_vma=False)
```

```python
import math

import jax
import jax.numpy as jnp
from jax import lax
from jax.experimental import pallas as pl
from jax.experimental.pallas import tpu as pltpu
from jax.sharding import PartitionSpec as P

MESH = pl.DeviceIdType.MESH
TERMS = 6
STEPS = 4
FINE = 1.0 / STEPS
NF = 9
NM = 56
NB = 21
PB = 24
LN = 128
F32 = jnp.float32
B16 = jnp.bfloat16


def coefficients(lower, upper):
    return [(upper ** (k + 1) - lower ** (k + 1)) / math.factorial(k + 1) for k in range(TERMS)]


FAST = coefficients(0.0, FINE)
WHOLE = coefficients(0.0, 1.0)
SLOW = [coefficients(s * FINE, (s + 1) * FINE) for s in range(STEPS)]


def two(x):
    high = x.astype(B16)
    return high, (x - high.astype(F32)).astype(B16)


def nn(a, b):
    return jnp.dot(a, b, preferred_element_type=F32)


def nt(a, b):
    return lax.dot_general(a, b, (((1,), (1,)), ((), ())), preferred_element_type=F32)


def stack3(x):
    high, low = two(x)
    return jnp.concatenate([high, low, high], axis=0)


def left3(x):
    high, low = two(x)
    return jnp.concatenate([high, high, low], axis=1)


def rows64(x):
    return jnp.concatenate([x, jnp.zeros((64 - NM, LN), F32)], axis=0)


def iota(shape, dim):
    return lax.broadcasted_iota(jnp.int32, shape, dim).astype(F32)


def hot(mask):
    return jnp.where(mask, 1.0, 0.0)


def pick(a, cm2):
    high, low = two(a)
    return nt(high, cm2) + nt(low, cm2)


def kernel(
    y_in, star_in, ds_in, vs_in, fp_in, fl_in, fa_in, cl_in, pa_in, ss_in, o_ref,
    y_ref, star_ref, ds_ref, vs_ref, fp_ref, fl_ref, fa_ref, cl_ref, pa_ref, ss_ref, insem,
    A3, V3, P3, PT3, PF, AF, X9, Xp, T9, Tp, TR9, TRp, SF, SS, CE, CO, STARF, FLF, FAF, Yp, Sp, SB, MF, Z9, Zp, Tq, U9, WK,
    send3, recv3, send, recv, ssem3, rsem3, ssem, rsem,
):
    loads = [
        pltpu.make_async_copy(a, b, insem.at[i])
        for i, (a, b) in enumerate((
            (fp_in, fp_ref), (y_in, y_ref), (fa_in, fa_ref), (cl_in, cl_ref), (ss_in, ss_ref),
            (ds_in, ds_ref), (vs_in, vs_ref), (pa_in, pa_ref), (star_in, star_ref), (fl_in, fl_ref),
        ))
    ]
    for load in loads:
        load.start()
    place = [lax.axis_index(a) for a in ("gx", "gy", "gz")]
    sizes = [lax.axis_size(a) for a in ("gx", "gy", "gz")]
    sides = []
    for d in range(6):
        axis, up = d // 2, d % 2
        there = place[axis] < sizes[axis] - 1 if up else place[axis] > 0
        target = list(place)
        target[axis] = place[axis] + (1 if up else -1)
        sides.append((there, tuple(target)))
    peers = sum(there.astype(jnp.int32) for there, _ in sides)

    barrier = pltpu.get_barrier_semaphore()
    for there, target in sides:
        @pl.when(there)
        def _():
            pl.semaphore_signal(barrier, inc=1, device_id=target, device_id_type=MESH)

    def link(s, d, arriving):
        to = d if arriving else d ^ 1
        target = sides[d][1]
        if s == STEPS - 1:
            pairs = [(send3.at[h, d], recv3.at[h, to], ssem3.at[h, d], rsem3.at[h, to]) for h in range(2)]
        else:
            pairs = [(send.at[s, d], recv.at[s, to], ssem.at[s, d], rsem.at[s, to])]
        return [
            pltpu.make_async_remote_copy(
                src_ref=a, dst_ref=b, send_sem=c, recv_sem=e, device_id=target, device_id_type=MESH)
            for a, b, c, e in pairs
        ]

    def start_all(s):
        for d in (5, 4, 1, 0, 3, 2):
            @pl.when(sides[d][0])
            def _():
                for copy in link(s, d, False):
                    copy.start()

    def arrive_all(s, which=range(6)):
        for d in which:
            @pl.when(sides[d][0])
            def _():
                for copy in link(s, d, True):
                    copy.wait_recv()

    def sent_all(s):
        for d in range(6):
            @pl.when(sides[d][0])
            def _():
                for copy in link(s, d, False):
                    copy.wait_send()

    low_half = lax.broadcasted_iota(jnp.int32, (1, LN), 1) < 64

    for load in loads[0:5]:
        load.wait()
    for b in range(NB):
        PF[b * 4 : b * 4 + 4, 0:NM] = fp_ref[b]
    pad = jnp.zeros((PB - NB, NM), F32)
    pf = jnp.concatenate(
        [r for c in range(4) for r in (PF[pl.ds(c, NB, stride=4), 0:NM], pad)], axis=0
    )
    pf = jnp.concatenate([pf, jnp.zeros((4 * PB, 64 - NM), F32)], axis=1)
    P3[...] = left3(pf)
    SF[NF * PB : 256, :] = jnp.zeros((256 - NF * PB, 512), F32)
    SS[NF * PB : 256, :] = jnp.zeros((256 - NF * PB, 256), F32)
    for f in range(NF):
        X9[:, f * LN : (f + 1) * LN] = stack3(rows64(y_ref[f]))
    TR9[...] = nn(P3[...], X9[...])

    def flux_full(ref, emit):
        for c in range(4):
            acc = [None] * NF
            for f in range(NF):
                t = TR9[c * PB : (c + 1) * PB, f * LN : (f + 1) * LN]
                for g in range(NF):
                    p = ref[g, f, c : c + 1, :] * t
                    acc[g] = p if acc[g] is None else acc[g] + p
            for g in range(NF):
                emit(c, g, acc[g])

    def put_sent(c, g, value):
        SF[g * PB : (g + 1) * PB, c * LN : (c + 1) * LN] = value

    flux_full(fa_ref, put_sent)

    fast = hot(cl_ref[...] == 0)
    fast512 = jnp.concatenate([fast] * 4, axis=1)
    slow512 = 1.0 - fast512
    eye = iota((32, 32), 0) == iota((32, 32), 1)
    lane512 = iota((32, 512), 1)
    parts = []
    for d in range(6):
        row = ss_ref[d : d + 1, :].astype(F32)
        column = jnp.sum(jnp.where(eye, row, 0.0), axis=1, keepdims=True)
        parts.append(hot(lane512 == column))
    slots = jnp.concatenate(parts, axis=0).astype(B16)
    flags = nt(jnp.broadcast_to(fast512, (16, 512)).astype(B16), slots)
    i_sub, i_lane = lax.broadcasted_iota(jnp.int32, (192, 192), 0), lax.broadcasted_iota(jnp.int32, (192, 192), 1)
    earlier = hot(jnp.logical_and(i_sub // 32 == i_lane // 32, i_sub < i_lane)).astype(B16)
    ranks = nn(flags.astype(B16), earlier)[0:1, :]
    flags = flags[0:1, :]
    lane192 = lax.broadcasted_iota(jnp.int32, (1, 192), 1)
    j_row = (lane192 % 32).astype(F32)
    position = jnp.where(flags > 0.5, ranks, 31.0 - (j_row - ranks))
    row_of = (lane192 // 32).astype(F32) * 16.0 + position + jnp.where(position > 15.5, 80.0, 0.0)
    moved = hot(i_sub.astype(F32) == row_of)
    j_column = jnp.sum(moved * j_row, axis=1, keepdims=True)
    fast_column = jnp.sum(moved * flags, axis=1, keepdims=True)
    ordered = nn(moved.astype(B16), slots).astype(B16)

    sent_hi, sent_lo = two(SF[...])
    out3 = nt(ordered, sent_hi) + nt(ordered, sent_lo)
    out3 = out3 + jnp.where(lax.broadcasted_iota(jnp.int32, (192, 256), 1) == 216, j_column, 0.0)
    for half in range(2):
        for d in range(6):
            r = half * 96 + d * 16
            send3[half, d] = out3[r : r + 16, :]
    send_constant = out3[0:96, :] * (1.0 - fast_column[0:96, :])

    pl.semaphore_wait(barrier, peers)
    start_all(STEPS - 1)

    for d in range(6):
        there, _ = sides[d]

        @pl.when(jnp.logical_not(there))
        def _():
            for half in range(2):
                recv3[half, d] = jnp.zeros((16, 256), F32)
            for s in range(STEPS - 1):
                recv[s, d] = jnp.zeros((16, 256), F32)

    for load in loads[5:]:
        load.wait()
    AF[...] = jnp.zeros(AF.shape, F32)
    for d in range(3):
        AF[d * NM : (d + 1) * NM, 0:NM] = jnp.transpose(ds_ref[d])
    A3[...] = left3(AF[:, 0:64])
    for d in range(3):
        AF[d * NM : (d + 1) * NM, 0:NM] = jnp.transpose(vs_ref[d])
    V3[...] = left3(AF[:, 0:64])
    PT3[...] = left3(jnp.transpose(pf))

    before = hot(iota((LN, LN), 0) < iota((LN, LN), 1)).astype(B16)
    rank = nn(jnp.broadcast_to(fast, (16, LN)).astype(B16), before)[0:1, :]
    sub = iota((LN, LN), 0)
    cm2 = jnp.concatenate([hot(sub == rank) * fast, hot(sub == rank + 64.0) * fast], axis=1).astype(B16)

    def compact_mats(ref, lead, out):
        CE[...] = jnp.zeros(CE.shape, F32)
        CO[...] = jnp.zeros(CO.shape, F32)
        for g in range(NF):
            for k in range(5):
                r = (g * 5 + k) * 4
                CE[r : r + lead, :] = ref[g, k]
                if k < 4:
                    CO[r : r + lead, :] = ref[g, k + 5]
                elif lead == 3:
                    CO[r : r + 1, :] = ref[g, 4, 1:2, :]
        out[...] = pick(jnp.concatenate([CE[...], CO[...]], axis=1), cm2)

    compact_mats(star_ref, 3, STARF)
    compact_mats(fl_ref, 4, FLF)
    compact_mats(fa_ref, 4, FAF)

    def second(k):
        return k + 5 if k < 4 else 4

    for k in range(5):
        Yp[:, k * LN : (k + 1) * LN] = pick(jnp.concatenate([y_ref[k], y_ref[second(k)]], axis=1), cm2)

    partner = jnp.concatenate([pa_ref[c : c + 1, :] for c in range(4)], axis=1).astype(F32)
    local = hot(iota((512, 512), 0) == partner).astype(B16)
    local_fast = jnp.concatenate(
        [nn(cm2, local[0:256, :]), nn(cm2, local[256:512, :])], axis=0
    ).astype(B16)

    def to_fast(a):
        return jnp.concatenate([nt(a[:, 0:256], cm2), nt(a[:, 256:512], cm2)], axis=1).astype(B16)

    local_ff = to_fast(local_fast)
    local_fs = (local_fast.astype(F32) * slow512).astype(B16)
    ordered_fast = to_fast(ordered[0:96, :])

    slow_hi = (sent_hi.astype(F32) * slow512).astype(B16)[0:224, :]
    slow_lo = (sent_lo.astype(F32) * slow512).astype(B16)[0:224, :]
    constant = nn(slow_hi, local) + nn(slow_lo, local)
    for i in range(2):
        cols = slice(i * 256, (i + 1) * 256)
        SS[:, i * LN : (i + 1) * LN] = nt(sent_hi[:, cols], cm2) + nt(sent_lo[:, cols], cm2)

    def put_own(c, g, value):
        Z9[c * PB : (c + 1) * PB, g * LN : (g + 1) * LN] = value

    flux_full(fl_ref, put_own)

    def star_full(T, emit):
        for base in (0, 3, 6):
            acc = [None] * 3
            for f in range(NF):
                for d in range(3):
                    t = T[d * NM : (d + 1) * NM, f * LN : (f + 1) * LN]
                    for q in range(3):
                        p = star_ref[base + q, f, d : d + 1, :] * t
                        acc[q] = p if acc[q] is None else acc[q] + p
            emit(base, acc)

    T9[...] = nn(V3[...], X9[...])

    def put_base(base, values):
        for q in range(3):
            SB[:, (base + q) * LN : (base + q + 1) * LN] = values[q]

    star_full(T9, put_base)

    def place_all(got, add):
        for c in range(4):
            for g in range(NF):
                value = got[g * PB : (g + 1) * PB, c * LN : (c + 1) * LN]
                at = (slice(c * PB, (c + 1) * PB), slice(g * LN, (g + 1) * LN))
                if add:
                    Z9[at] += value
                else:
                    Z9[at] = value

    place_all(constant, True)
    SB[...] += nn(PT3[...], stack3(Z9[...]))[0:NM, :]
    for k in range(5):
        Sp[:, k * LN : (k + 1) * LN] = pick(
            jnp.concatenate([SB[:, k * LN : (k + 1) * LN], SB[:, second(k) * LN : (second(k) + 1) * LN]], axis=1), cm2
        )
    slow128 = 1.0 - fast
    for g in range(NF):
        SB[:, g * LN : (g + 1) * LN] = SB[:, g * LN : (g + 1) * LN] * slow128

    def turned(a):
        return two(jnp.transpose(a)[0:224, :])

    def remote_slots(rows, dirs):
        n = len(dirs) * 16
        row = lax.broadcasted_iota(jnp.int32, (2 * n, 1), 0)
        side = ((row % n) // 16 + dirs[0]).astype(F32)
        return hot(partner == 512.0 + side * 32.0 + rows[:, 216:217]).astype(B16)

    def masked(a):
        return (a.astype(F32) * slow512).astype(B16)

    def star_fast(T, emit):
        for block in ((0, 5, 1, 6), (2, 7, 3, 8), (4,)):
            acc = [None] * len(block)

            def add(q, row, t):
                p = STARF[row : row + 1, :] * t
                acc[q] = p if acc[q] is None else acc[q] + p

            for k in range(4):
                for d in range(3):
                    t = T[d * NM : (d + 1) * NM, k * LN : (k + 1) * LN]
                    for q, g in enumerate(block):
                        add(q, (g * 5 + k) * 4 + d, t)
            last = slice(4 * LN, 5 * LN)
            t01 = jnp.where(low_half, T[0:NM, last], T[NM : 2 * NM, last])
            t2 = T[2 * NM : 3 * NM, last]
            for q, g in enumerate(block):
                add(q, (g * 5 + 4) * 4, t01)
                add(q, (g * 5 + 4) * 4 + 2, t2)
            if len(block) == 1:
                emit(4, acc[0] + pltpu.roll(acc[0], 64, 1))
            else:
                for q in (0, 2):
                    emit(block[q], halves(acc[q], acc[q + 1]))

    def halves(a, b):
        return jnp.where(low_half, a, b) + pltpu.roll(jnp.where(low_half, b, a), 64, 1)

    def flux_fast(ref, c):
        acc = [None] * NF
        for k in range(5):
            t = TRp[c * PB : (c + 1) * PB, k * LN : (k + 1) * LN]
            for g in range(NF):
                r = (g * 5 + k) * 4 + c
                p = ref[r : r + 1, :] * t
                acc[g] = p if acc[g] is None else acc[g] + p
        return acc

    def put_x(k, value):
        Xp[:, k * LN : (k + 1) * LN] = stack3(rows64(value))

    def arrange(a, add):
        for k in range(5):
            for i in range(2):
                e = a[k * PB : (k + 1) * PB, i * LN : (i + 1) * LN]
                o = a[second(k) * PB : (second(k) + 1) * PB, i * LN : (i + 1) * LN]
                c = 2 * i
                v0 = jnp.where(low_half, e, pltpu.roll(o, 64, 1))
                v1 = jnp.where(low_half, pltpu.roll(e, 64, 1), o)
                cols = slice(k * LN, (k + 1) * LN)
                if add:
                    Zp[c * PB : (c + 1) * PB, cols] += v0
                    Zp[(c + 1) * PB : (c + 2) * PB, cols] += v1
                else:
                    Zp[c * PB : (c + 1) * PB, cols] = v0
                    Zp[(c + 1) * PB : (c + 2) * PB, cols] = v1

    def multiply(T, first, values):
        x = jnp.concatenate([stack3(rows64(v)) for v in values], axis=1)
        T[:, first * LN : (first + len(values)) * LN] = nn(A3[...], x)

    def fast_level(T, c, out):
        held = []

        def emit(k, value):
            held.append(value + c * Sp[:, k * LN : (k + 1) * LN])
            if k in (1, 3, 4):
                multiply(out, k + 1 - len(held), held)
                held.clear()

        star_fast(T, emit)

    def horner_fast():
        for group in ((0, 1), (2, 3), (4,)):
            multiply(Tp, group[0], [FAST[TERMS - 1] * Sp[:, k * LN : (k + 1) * LN] for k in group])

        def levels(i, c):
            k = (TERMS - 1 - 2 * i).astype(F32)
            fast_level(Tp, c, Tq)
            c = c * (k * (1.0 / FINE))
            fast_level(Tq, c, Tp)
            return c * ((k - 1.0) * (1.0 / FINE))

        lax.fori_loop(0, (TERMS - 2) // 2, levels, jnp.float32(FAST[TERMS - 2]))

        def emit(k, value):
            cols = slice(k * LN, (k + 1) * LN)
            value = Yp[:, cols] + (value + FAST[0] * Sp[:, cols])
            Yp[:, cols] = value
            put_x(k, value)

        star_fast(Tp, emit)

    def gather(pairs):
        total = None
        for high, low, ones in pairs:
            got = nn(high, ones) + nn(low, ones)
            total = got if total is None else total + got
        return total

    def slow_source(s, got):
        place_all(got, False)
        MF[s] = nn(PT3[...], stack3(Z9[...]))[0:NM, :]

    def twice(pair):
        return jnp.concatenate(pair, axis=1)

    hi, lo = two(SS[...])
    hi, lo = hi[0:224, :], lo[0:224, :]
    local_part = gather([(hi, lo, local_ff)])
    arrange(local_part, False)
    waiting = [(hi, lo, local_fs)]
    late = []
    later = []
    for dirs in ((0, 1, 2, 3), (4, 5)):
        n = 16 * len(dirs)
        arrive_all(STEPS - 1, dirs)
        rows = jnp.concatenate([recv3[half, d] for half in range(2) for d in dirs], axis=0)
        remote = remote_slots(rows, dirs)
        remote_ff = to_fast(remote)
        r_hi, r_lo = turned(rows)
        arrange(gather([(r_hi, r_lo, remote_ff)]), dirs[0] == 0)
        Sp[...] += nn(PT3[...], stack3(Zp[...]))[0:NM, :]
        late.append((rows, remote, n))
        later.append((remote_ff[0:n, :], remote))
    horner_fast()
    near_ff = later[0][0]
    far_ff = jnp.concatenate([later[1][0]] * 2, axis=0)
    far_all = jnp.concatenate([later[1][1][0:32, :]] * 2, axis=0)

    for s in range(STEPS - 2, -1, -1):
        TRp[...] = nn(P3[...], Xp[...])
        for i in range(2):
            a0, a1 = flux_fast(FAF, 2 * i), flux_fast(FAF, 2 * i + 1)
            for g in range(NF):
                SS[g * PB : (g + 1) * PB, i * LN : (i + 1) * LN] = halves(a0[g], a1[g])
        hi, lo = two(SS[...])
        out = nt(ordered_fast, hi) + nt(ordered_fast, lo) + send_constant
        for d in range(6):
            send[s, d] = out[d * 16 : (d + 1) * 16, :]
        start_all(s)

        hi, lo = hi[0:224, :], lo[0:224, :]
        Tp[...] = nn(V3[...], Xp[...])

        def put_source(k, value):
            Sp[:, k * LN : (k + 1) * LN] = value

        star_fast(Tp, put_source)
        for c in range(4):
            acc = flux_fast(FLF, c)
            for k in range(5):
                value = halves(acc[k], acc[k + 5]) if k < 4 else acc[4] + pltpu.roll(acc[4], 64, 1)
                Zp[c * PB : (c + 1) * PB, k * LN : (k + 1) * LN] = value
        if s == STEPS - 2:
            terms = []
            for rows, remote, n in late:
                r_hi, r_lo = turned(rows[0:n, :])
                waiting.append((r_hi, r_lo, masked(remote[0:n, :])))
                r_hi, r_lo = turned(rows[n : 2 * n, :])
                terms.append((r_hi, r_lo, remote[n : 2 * n, :]))
            extra = gather(terms)
            constant_fast = pick_two(constant + extra, cm2)
            place_all(extra * slow512, False)
            SB[...] += nn(PT3[...], stack3(Z9[...]))[0:NM, :]
            near_fs, far_fs = masked(late[0][1][0:64, :]), masked(late[1][1][0:32, :])
        slow_source(s + 1, gather(waiting))

        arrive_all(s, (0, 1, 2, 3))
        r_hi, r_lo = turned(jnp.concatenate([recv[s, d] for d in range(4)], axis=0))
        arrange(gather([(hi, lo, local_ff), (r_hi, r_lo, near_ff)]) + constant_fast, True)
        Sp[...] += nn(PT3[...], stack3(Zp[...]))[0:NM, :]
        waiting = [(hi, lo, local_fs), (r_hi, r_lo, near_fs)]
        if s == 0:
            slow_source(0, gather(waiting))
            s_hi, s_lo = two(Sp[...])
            y_hi, y_lo = two(Yp[...])
            for k in range(5):
                cols = slice(k * LN, (k + 1) * LN)
                source = nn(s_hi[:, cols], cm2) + nn(s_lo[:, cols], cm2)
                value = nn(y_hi[:, cols], cm2) + nn(y_lo[:, cols], cm2)
                for q, f in enumerate((k, k + 5) if k < 4 else (4,)):
                    MF[0, :, f * LN : (f + 1) * LN] += source[:, q * LN : (q + 1) * LN]
                    o_ref[f] = value[:, q * LN : (q + 1) * LN] + y_ref[f] * slow128
            for g in range(NF):
                cols = slice(g * LN, (g + 1) * LN)
                base, parts = SB[:, cols], [MF[q, :, cols] for q in range(STEPS)]
                for k in range(TERMS):
                    total = WHOLE[k] * base
                    for q in range(STEPS):
                        total = total + SLOW[q][k] * parts[q]
                    WK[k, :, cols] = total

        arrive_all(s, (4, 5))
        far = jnp.concatenate(turned(jnp.concatenate([recv[s, d] for d in (4, 5)], axis=0)), axis=1)
        if s > 0:
            arrange(nn(far, far_ff), False)
            Sp[...] += nn(PT3[...], stack3(Zp[...]))[0:NM, :]
            horner_fast()
            waiting.append((far[:, 0:32], far[:, 32:64], far_fs))
        else:
            slow_source(0, nn(far, far_all))

    def weighted(k, g):
        cols = slice(g * LN, (g + 1) * LN)
        return WK[k, :, cols] + SLOW[0][k] * MF[0, :, cols]

    for base in (0, 3, 6):
        multiply(T9, base, [weighted(TERMS - 1, base + q) for q in range(3)])
    here, there = T9, U9
    for k in range(TERMS - 2, -1, -1):
        def emit(base, values):
            totals = [values[q] + weighted(k, base + q) for q in range(3)]
            if k > 0:
                multiply(there, base, totals)
            else:
                for q in range(3):
                    o_ref[base + q] += totals[q]

        star_full(here, emit)
        here, there = there, here

    for s in range(STEPS):
        sent_all(s)


def pick_two(a, cm2):
    return jnp.concatenate([pick(a[:, 0:256], cm2), pick(a[:, 256:512], cm2)], axis=1)


def body(
    final_adjoint, star_mats, deriv_stiff, volume_stiffness, face_projection,
    flux_local, flux_across, cluster, partner, send_slots,
):
    V = pltpu.VMEM
    D = pltpu.SemaphoreType.DMA
    views = (
        final_adjoint, jnp.transpose(star_mats, (1, 2, 0, 3)), deriv_stiff, volume_stiffness,
        jnp.transpose(face_projection, (1, 0, 2)), jnp.transpose(flux_local, (1, 2, 0, 3)),
        jnp.transpose(flux_across, (1, 2, 0, 3)), cluster.reshape(1, LN), partner, send_slots,
    )
    scratch = [V(a.shape, a.dtype) for a in views] + [
        D((10,)),
        V((168, 192), B16), V((168, 192), B16), V((96, 192), B16), V((64, 288), B16), V((96, LN), F32), V((168, LN), F32),
        V((192, 1152), B16), V((192, 640), B16), V((168, 1152), F32), V((168, 640), F32), V((96, 1152), F32), V((96, 640), F32),
        V((256, 512), F32), V((256, 256), F32), V((184, LN), F32), V((184, LN), F32),
        V((184, LN), F32), V((184, LN), F32), V((184, LN), F32),
        V((NM, 640), F32), V((NM, 640), F32), V((NM, 1152), F32), V((STEPS, NM, 1152), F32),
        V((96, 1152), F32), V((96, 640), F32), V((168, 640), F32), V((168, 1152), F32), V((TERMS, NM, 1152), F32),
        V((2, 6, 16, 256), F32), V((2, 6, 16, 256), F32),
        V((STEPS - 1, 6, 16, 256), F32), V((STEPS - 1, 6, 16, 256), F32),
        D((2, 6)), D((2, 6)), D((STEPS - 1, 6)), D((STEPS - 1, 6)),
    ]
    return pl.pallas_call(
        kernel,
        out_shape=jax.ShapeDtypeStruct(final_adjoint.shape, F32),
        in_specs=[pl.BlockSpec(memory_space=pltpu.HBM)] * 10,
        out_specs=pl.BlockSpec(memory_space=pltpu.VMEM),
        scratch_shapes=scratch,
        compiler_params=pltpu.CompilerParams(collective_id=0, has_side_effects=True, vmem_limit_bytes=64 * 2**20),
        name="coarse_step",
    )(*views)


def solution(mesh):
    every = ("gx", "gy", "gz")
    in_specs = (
        P(None, None, every), P(None, None, None, every), P(), P(), P(),
        P(None, None, None, every), P(None, None, None, every), P(every), P(None, every), P(None, every),
    )
    return jax.shard_map(body, mesh=mesh, in_specs=in_specs, out_specs=P(None, None, every), check_vma=False)
```

```python
import math

import jax
import jax.numpy as jnp
from jax import lax
from jax.experimental import pallas as pl
from jax.experimental.pallas import tpu as pltpu
from jax.sharding import PartitionSpec as P

MESH = pl.DeviceIdType.MESH
TERMS = 6
STEPS = 4
FINE = 1.0 / STEPS
NF = 9
NM = 56
NB = 21
PB = 24
LN = 128
F32 = jnp.float32
B16 = jnp.bfloat16


def coefficients(lower, upper):
    return [(upper ** (k + 1) - lower ** (k + 1)) / math.factorial(k + 1) for k in range(TERMS)]


FAST = coefficients(0.0, FINE)
WHOLE = coefficients(0.0, 1.0)
SLOW = [coefficients(s * FINE, (s + 1) * FINE) for s in range(STEPS)]


def two(x):
    high = x.astype(B16)
    return high, (x - high.astype(F32)).astype(B16)


def nn(a, b):
    return jnp.dot(a, b, preferred_element_type=F32)


def nt(a, b):
    return lax.dot_general(a, b, (((1,), (1,)), ((), ())), preferred_element_type=F32)


def stack3(x):
    high, low = two(x)
    return jnp.concatenate([high, low, high], axis=0)


def left3(x):
    high, low = two(x)
    return jnp.concatenate([high, high, low], axis=1)


def rows64(x):
    return jnp.concatenate([x, jnp.zeros((64 - NM, LN), F32)], axis=0)


def iota(shape, dim):
    return lax.broadcasted_iota(jnp.int32, shape, dim).astype(F32)


def hot(mask):
    return jnp.where(mask, 1.0, 0.0)


def pick(a, cm2):
    high, low = two(a)
    return nt(high, cm2) + nt(low, cm2)


def kernel(
    y_in, star_in, ds_in, vs_in, fp_in, fl_in, fa_in, cl_in, pa_in, ss_in, o_out,
    y_ref, star_ref, ds_ref, vs_ref, fp_ref, fl_ref, fa_ref, cl_ref, pa_ref, ss_ref, insem, o_ref, osem,
    A3, V3, P3, PT3, PF, AF, X9, Xp, T9, Tp, TR9, TRp, SF, SS, CE, CO, STARF, FLF, FAF, Yp, Sp, SB, MF, Z9, Zp, Tq, U9, WK,
    send3, recv3, send, recv, ssem3, rsem3, ssem, rsem,
):
    loads = [
        pltpu.make_async_copy(a, b, insem.at[i])
        for i, (a, b) in enumerate((
            (fp_in, fp_ref), (y_in, y_ref), (fa_in, fa_ref), (cl_in, cl_ref), (ss_in, ss_ref),
            (ds_in, ds_ref), (vs_in, vs_ref), (pa_in, pa_ref), (star_in, star_ref), (fl_in, fl_ref),
        ))
    ]
    place = [lax.axis_index(a) for a in ("gx", "gy", "gz")]
    sizes = [lax.axis_size(a) for a in ("gx", "gy", "gz")]
    sides = []
    for d in range(6):
        axis, up = d // 2, d % 2
        there = place[axis] < sizes[axis] - 1 if up else place[axis] > 0
        target = list(place)
        target[axis] = place[axis] + (1 if up else -1)
        sides.append((there, tuple(target)))
    peers = sum(there.astype(jnp.int32) for there, _ in sides)

    barrier = pltpu.get_barrier_semaphore()
    for there, target in sides[::-1]:
        @pl.when(there)
        def _():
            pl.semaphore_signal(barrier, inc=1, device_id=target, device_id_type=MESH)

    for load in loads:
        load.start()

    def link(s, d, arriving):
        to = d if arriving else d ^ 1
        target = sides[d][1]
        if s == STEPS - 1:
            pairs = [(send3.at[h, d], recv3.at[h, to], ssem3.at[h, d], rsem3.at[h, to]) for h in range(2)]
        else:
            pairs = [(send.at[s, d], recv.at[s, to], ssem.at[s, d], rsem.at[s, to])]
        return [
            pltpu.make_async_remote_copy(
                src_ref=a, dst_ref=b, send_sem=c, recv_sem=e, device_id=target, device_id_type=MESH)
            for a, b, c, e in pairs
        ]

    def start_all(s):
        for d in (5, 4, 1, 0, 3, 2):
            @pl.when(sides[d][0])
            def _():
                for copy in link(s, d, False):
                    copy.start()

    def arrive_all(s, which=range(6)):
        for d in which:
            @pl.when(sides[d][0])
            def _():
                for copy in link(s, d, True):
                    copy.wait_recv()

    def sent_all(s):
        for d in range(6):
            @pl.when(sides[d][0])
            def _():
                for copy in link(s, d, False):
                    copy.wait_send()

    low_half = lax.broadcasted_iota(jnp.int32, (1, LN), 1) < 64

    for load in loads[0:5]:
        load.wait()
    for b in range(NB):
        PF[b * 4 : b * 4 + 4, 0:NM] = fp_ref[b]
    pad = jnp.zeros((PB - NB, NM), F32)
    pf = jnp.concatenate(
        [r for c in range(4) for r in (PF[pl.ds(c, NB, stride=4), 0:NM], pad)], axis=0
    )
    pf = jnp.concatenate([pf, jnp.zeros((4 * PB, 64 - NM), F32)], axis=1)
    P3[...] = left3(pf)
    SF[NF * PB : 256, :] = jnp.zeros((256 - NF * PB, 512), F32)
    SS[NF * PB : 256, :] = jnp.zeros((256 - NF * PB, 256), F32)
    for f in range(NF):
        X9[:, f * LN : (f + 1) * LN] = stack3(rows64(y_ref[f]))
    TR9[...] = nn(P3[...], X9[...])

    def flux_full(ref, emit):
        for c in range(4):
            acc = [None] * NF
            for f in range(NF):
                t = TR9[c * PB : (c + 1) * PB, f * LN : (f + 1) * LN]
                for g in range(NF):
                    p = ref[g, f, c : c + 1, :] * t
                    acc[g] = p if acc[g] is None else acc[g] + p
            for g in range(NF):
                emit(c, g, acc[g])

    def put_sent(c, g, value):
        SF[g * PB : (g + 1) * PB, c * LN : (c + 1) * LN] = value

    flux_full(fa_ref, put_sent)

    fast = hot(cl_ref[...] == 0)
    fast512 = jnp.concatenate([fast] * 4, axis=1)
    slow512 = 1.0 - fast512
    eye = iota((32, 32), 0) == iota((32, 32), 1)
    lane512 = iota((32, 512), 1)
    parts = []
    for d in range(6):
        row = ss_ref[d : d + 1, :].astype(F32)
        column = jnp.sum(jnp.where(eye, row, 0.0), axis=1, keepdims=True)
        parts.append(hot(lane512 == column))
    slots = jnp.concatenate(parts, axis=0).astype(B16)
    flags = nt(jnp.broadcast_to(fast512, (16, 512)).astype(B16), slots)
    i_sub, i_lane = lax.broadcasted_iota(jnp.int32, (192, 192), 0), lax.broadcasted_iota(jnp.int32, (192, 192), 1)
    earlier = hot(jnp.logical_and(i_sub // 32 == i_lane // 32, i_sub < i_lane)).astype(B16)
    ranks = nn(flags.astype(B16), earlier)[0:1, :]
    flags = flags[0:1, :]
    lane192 = lax.broadcasted_iota(jnp.int32, (1, 192), 1)
    j_row = (lane192 % 32).astype(F32)
    position = jnp.where(flags > 0.5, ranks, 31.0 - (j_row - ranks))
    row_of = (lane192 // 32).astype(F32) * 16.0 + position + jnp.where(position > 15.5, 80.0, 0.0)
    moved = hot(i_sub.astype(F32) == row_of)
    j_column = jnp.sum(moved * j_row, axis=1, keepdims=True)
    fast_column = jnp.sum(moved * flags, axis=1, keepdims=True)
    ordered = nn(moved.astype(B16), slots).astype(B16)

    sent_hi, sent_lo = two(SF[...])
    out3 = nt(ordered, sent_hi) + nt(ordered, sent_lo)
    out3 = out3 + jnp.where(lax.broadcasted_iota(jnp.int32, (192, 256), 1) == 216, j_column, 0.0)
    for half in range(2):
        for d in range(6):
            r = half * 96 + d * 16
            send3[half, d] = out3[r : r + 16, :]
    send_constant = out3[0:96, :] * (1.0 - fast_column[0:96, :])

    pl.semaphore_wait(barrier, peers)
    start_all(STEPS - 1)

    for d in range(6):
        there, _ = sides[d]

        @pl.when(jnp.logical_not(there))
        def _():
            for half in range(2):
                recv3[half, d] = jnp.zeros((16, 256), F32)
            for s in range(STEPS - 1):
                recv[s, d] = jnp.zeros((16, 256), F32)

    for load in loads[5:]:
        load.wait()
    AF[...] = jnp.zeros(AF.shape, F32)
    for d in range(3):
        AF[d * NM : (d + 1) * NM, 0:NM] = jnp.transpose(ds_ref[d])
    A3[...] = left3(AF[:, 0:64])
    for d in range(3):
        AF[d * NM : (d + 1) * NM, 0:NM] = jnp.transpose(vs_ref[d])
    V3[...] = left3(AF[:, 0:64])
    PT3[...] = left3(jnp.transpose(pf))

    before = hot(iota((LN, LN), 0) < iota((LN, LN), 1)).astype(B16)
    rank = nn(jnp.broadcast_to(fast, (16, LN)).astype(B16), before)[0:1, :]
    sub = iota((LN, LN), 0)
    cm2 = jnp.concatenate([hot(sub == rank) * fast, hot(sub == rank + 64.0) * fast], axis=1).astype(B16)

    def compact_mats(ref, lead, out):
        CE[...] = jnp.zeros(CE.shape, F32)
        CO[...] = jnp.zeros(CO.shape, F32)
        for g in range(NF):
            for k in range(5):
                r = (g * 5 + k) * 4
                CE[r : r + lead, :] = ref[g, k]
                if k < 4:
                    CO[r : r + lead, :] = ref[g, k + 5]
                elif lead == 3:
                    CO[r : r + 1, :] = ref[g, 4, 1:2, :]
        out[...] = pick(jnp.concatenate([CE[...], CO[...]], axis=1), cm2)

    compact_mats(star_ref, 3, STARF)
    compact_mats(fl_ref, 4, FLF)
    compact_mats(fa_ref, 4, FAF)

    def second(k):
        return k + 5 if k < 4 else 4

    for k in range(5):
        Yp[:, k * LN : (k + 1) * LN] = pick(jnp.concatenate([y_ref[k], y_ref[second(k)]], axis=1), cm2)

    partner = jnp.concatenate([pa_ref[c : c + 1, :] for c in range(4)], axis=1).astype(F32)
    local = hot(iota((512, 512), 0) == partner).astype(B16)
    local_fast = jnp.concatenate(
        [nn(cm2, local[0:256, :]), nn(cm2, local[256:512, :])], axis=0
    ).astype(B16)

    def to_fast(a):
        return jnp.concatenate([nt(a[:, 0:256], cm2), nt(a[:, 256:512], cm2)], axis=1).astype(B16)

    local_ff = to_fast(local_fast)
    local_fs = (local_fast.astype(F32) * slow512).astype(B16)
    ordered_fast = to_fast(ordered[0:96, :])

    slow_hi = (sent_hi.astype(F32) * slow512).astype(B16)[0:224, :]
    slow_lo = (sent_lo.astype(F32) * slow512).astype(B16)[0:224, :]
    constant = nn(slow_hi, local) + nn(slow_lo, local)
    for i in range(2):
        cols = slice(i * 256, (i + 1) * 256)
        SS[:, i * LN : (i + 1) * LN] = nt(sent_hi[:, cols], cm2) + nt(sent_lo[:, cols], cm2)

    def put_own(c, g, value):
        Z9[c * PB : (c + 1) * PB, g * LN : (g + 1) * LN] = value

    flux_full(fl_ref, put_own)

    def star_full(T, emit):
        for base in (0, 3, 6):
            acc = [None] * 3
            for f in range(NF):
                for d in range(3):
                    t = T[d * NM : (d + 1) * NM, f * LN : (f + 1) * LN]
                    for q in range(3):
                        p = star_ref[base + q, f, d : d + 1, :] * t
                        acc[q] = p if acc[q] is None else acc[q] + p
            emit(base, acc)

    T9[...] = nn(V3[...], X9[...])

    def put_base(base, values):
        for q in range(3):
            SB[:, (base + q) * LN : (base + q + 1) * LN] = values[q]

    star_full(T9, put_base)

    def place_all(got, add):
        for c in range(4):
            for g in range(NF):
                value = got[g * PB : (g + 1) * PB, c * LN : (c + 1) * LN]
                at = (slice(c * PB, (c + 1) * PB), slice(g * LN, (g + 1) * LN))
                if add:
                    Z9[at] += value
                else:
                    Z9[at] = value

    place_all(constant, True)
    SB[...] += nn(PT3[...], stack3(Z9[...]))[0:NM, :]
    for k in range(5):
        Sp[:, k * LN : (k + 1) * LN] = pick(
            jnp.concatenate([SB[:, k * LN : (k + 1) * LN], SB[:, second(k) * LN : (second(k) + 1) * LN]], axis=1), cm2
        )
    slow128 = 1.0 - fast
    for g in range(NF):
        SB[:, g * LN : (g + 1) * LN] = SB[:, g * LN : (g + 1) * LN] * slow128

    def turned(a):
        return two(jnp.transpose(a)[0:224, :])

    def remote_slots(rows, dirs):
        n = len(dirs) * 16
        row = lax.broadcasted_iota(jnp.int32, (2 * n, 1), 0)
        side = ((row % n) // 16 + dirs[0]).astype(F32)
        return hot(partner == 512.0 + side * 32.0 + rows[:, 216:217]).astype(B16)

    def masked(a):
        return (a.astype(F32) * slow512).astype(B16)

    def star_fast(T, emit):
        for block in ((0, 5, 1, 6), (2, 7, 3, 8), (4,)):
            acc = [None] * len(block)

            def add(q, row, t):
                p = STARF[row : row + 1, :] * t
                acc[q] = p if acc[q] is None else acc[q] + p

            for k in range(4):
                for d in range(3):
                    t = T[d * NM : (d + 1) * NM, k * LN : (k + 1) * LN]
                    for q, g in enumerate(block):
                        add(q, (g * 5 + k) * 4 + d, t)
            last = slice(4 * LN, 5 * LN)
            t01 = jnp.where(low_half, T[0:NM, last], T[NM : 2 * NM, last])
            t2 = T[2 * NM : 3 * NM, last]
            for q, g in enumerate(block):
                add(q, (g * 5 + 4) * 4, t01)
                add(q, (g * 5 + 4) * 4 + 2, t2)
            if len(block) == 1:
                emit(4, acc[0] + pltpu.roll(acc[0], 64, 1))
            else:
                for q in (0, 2):
                    emit(block[q], halves(acc[q], acc[q + 1]))

    def halves(a, b):
        return jnp.where(low_half, a, b) + pltpu.roll(jnp.where(low_half, b, a), 64, 1)

    def flux_fast(ref, c):
        acc = [None] * NF
        for k in range(5):
            t = TRp[c * PB : (c + 1) * PB, k * LN : (k + 1) * LN]
            for g in range(NF):
                r = (g * 5 + k) * 4 + c
                p = ref[r : r + 1, :] * t
                acc[g] = p if acc[g] is None else acc[g] + p
        return acc

    def put_x(k, value):
        Xp[:, k * LN : (k + 1) * LN] = stack3(rows64(value))

    def arrange(a, add):
        for k in range(5):
            for i in range(2):
                e = a[k * PB : (k + 1) * PB, i * LN : (i + 1) * LN]
                o = a[second(k) * PB : (second(k) + 1) * PB, i * LN : (i + 1) * LN]
                c = 2 * i
                v0 = jnp.where(low_half, e, pltpu.roll(o, 64, 1))
                v1 = jnp.where(low_half, pltpu.roll(e, 64, 1), o)
                cols = slice(k * LN, (k + 1) * LN)
                if add:
                    Zp[c * PB : (c + 1) * PB, cols] += v0
                    Zp[(c + 1) * PB : (c + 2) * PB, cols] += v1
                else:
                    Zp[c * PB : (c + 1) * PB, cols] = v0
                    Zp[(c + 1) * PB : (c + 2) * PB, cols] = v1

    def multiply(T, first, values):
        x = jnp.concatenate([stack3(rows64(v)) for v in values], axis=1)
        T[:, first * LN : (first + len(values)) * LN] = nn(A3[...], x)

    def fast_level(T, c, out):
        held = []

        def emit(k, value):
            held.append(value + c * Sp[:, k * LN : (k + 1) * LN])
            if k in (1, 3, 4):
                multiply(out, k + 1 - len(held), held)
                held.clear()

        star_fast(T, emit)

    def horner_fast():
        for group in ((0, 1), (2, 3), (4,)):
            multiply(Tp, group[0], [FAST[TERMS - 1] * Sp[:, k * LN : (k + 1) * LN] for k in group])

        here, there = Tp, Tq
        for k in range(TERMS - 2, 0, -1):
            fast_level(here, FAST[k], there)
            here, there = there, here

        def emit(k, value):
            cols = slice(k * LN, (k + 1) * LN)
            value = Yp[:, cols] + (value + FAST[0] * Sp[:, cols])
            Yp[:, cols] = value
            put_x(k, value)
            if k in (1, 3, 4):
                group = slice((k - k % 2 if k < 4 else 4) * LN, (k + 1) * LN)
                TRp[:, group] = nn(P3[...], Xp[:, group])

        star_fast(Tp, emit)

    def gather(pairs):
        total = None
        for high, low, ones in pairs:
            got = nn(high, ones) + nn(low, ones)
            total = got if total is None else total + got
        return total

    def slow_source(s, got):
        place_all(got, False)
        MF[s] = nn(PT3[...], stack3(Z9[...]))[0:NM, :]

    def twice(pair):
        return jnp.concatenate(pair, axis=1)

    hi, lo = two(SS[...])
    hi, lo = hi[0:224, :], lo[0:224, :]
    local_part = gather([(hi, lo, local_ff)])
    arrange(local_part, False)
    waiting = [(hi, lo, local_fs)]
    late = []
    later = []
    for dirs in ((0, 1, 2, 3), (4, 5)):
        n = 16 * len(dirs)
        arrive_all(STEPS - 1, dirs)
        rows = jnp.concatenate([recv3[half, d] for half in range(2) for d in dirs], axis=0)
        remote = remote_slots(rows, dirs)
        remote_ff = to_fast(remote)
        r_hi, r_lo = turned(rows)
        arrange(gather([(r_hi, r_lo, remote_ff)]), dirs[0] == 0)
        Sp[...] += nn(PT3[...], stack3(Zp[...]))[0:NM, :]
        late.append((rows, remote, n))
        later.append((remote_ff[0:n, :], remote))
    horner_fast()
    near_ff = later[0][0]
    far_slots = later[1][1][0:32, :]
    far_pairs = jnp.concatenate(
        [
            jnp.concatenate([nt(far_slots[:, c * LN : (c + 1) * LN], cm2[:, q * LN : (q + 1) * LN]) for c in range(4)], axis=1)
            for q in (0, 1, 0, 1)
        ],
        axis=0,
    ).astype(B16)
    far_all = jnp.concatenate([later[1][1][0:32, :]] * 2, axis=0)

    for s in range(STEPS - 2, -1, -1):
        for i in range(2):
            a0, a1 = flux_fast(FAF, 2 * i), flux_fast(FAF, 2 * i + 1)
            for g in range(NF):
                SS[g * PB : (g + 1) * PB, i * LN : (i + 1) * LN] = halves(a0[g], a1[g])
        hi, lo = two(SS[...])
        out = nt(ordered_fast, hi) + nt(ordered_fast, lo) + send_constant
        for d in range(6):
            send[s, d] = out[d * 16 : (d + 1) * 16, :]
        start_all(s)

        hi, lo = hi[0:224, :], lo[0:224, :]
        Tp[...] = nn(V3[...], Xp[...])

        def put_source(k, value):
            Sp[:, k * LN : (k + 1) * LN] = value

        star_fast(Tp, put_source)
        for c in range(4):
            acc = flux_fast(FLF, c)
            for k in range(5):
                value = halves(acc[k], acc[k + 5]) if k < 4 else acc[4] + pltpu.roll(acc[4], 64, 1)
                Zp[c * PB : (c + 1) * PB, k * LN : (k + 1) * LN] = value
        if s == STEPS - 2:
            terms = []
            for rows, remote, n in late:
                r_hi, r_lo = turned(rows[0:n, :])
                waiting.append((r_hi, r_lo, masked(remote[0:n, :])))
                r_hi, r_lo = turned(rows[n : 2 * n, :])
                terms.append((r_hi, r_lo, remote[n : 2 * n, :]))
            extra = gather(terms)
            constant_fast = pick_two(constant + extra, cm2)
            place_all(extra * slow512, False)
            SB[...] += nn(PT3[...], stack3(Z9[...]))[0:NM, :]
            near_fs, far_fs = masked(late[0][1][0:64, :]), masked(late[1][1][0:32, :])
        slow_source(s + 1, gather(waiting))

        arrive_all(s, (0, 1, 2, 3))
        r_hi, r_lo = turned(jnp.concatenate([recv[s, d] for d in range(4)], axis=0))
        arrange(gather([(hi, lo, local_ff), (r_hi, r_lo, near_ff)]) + constant_fast, True)
        Sp[...] += nn(PT3[...], stack3(Zp[...]))[0:NM, :]
        waiting = [(hi, lo, local_fs), (r_hi, r_lo, near_fs)]
        if s == 0:
            slow_source(0, gather(waiting))
            s_hi, s_lo = two(Sp[...])
            y_hi, y_lo = two(Yp[...])
            for k in range(5):
                cols = slice(k * LN, (k + 1) * LN)
                source = nn(s_hi[:, cols], cm2) + nn(s_lo[:, cols], cm2)
                value = nn(y_hi[:, cols], cm2) + nn(y_lo[:, cols], cm2)
                for q, f in enumerate((k, k + 5) if k < 4 else (4,)):
                    MF[0, :, f * LN : (f + 1) * LN] += source[:, q * LN : (q + 1) * LN]
                    o_ref[f] = value[:, q * LN : (q + 1) * LN] + y_ref[f] * slow128
            for g in range(NF):
                cols = slice(g * LN, (g + 1) * LN)
                base, parts = SB[:, cols], [MF[q, :, cols] for q in range(STEPS)]
                for k in range(TERMS):
                    total = WHOLE[k] * base
                    for q in range(STEPS):
                        total = total + SLOW[q][k] * parts[q]
                    WK[k, :, cols] = total

        arrive_all(s, (4, 5))
        came = jnp.concatenate([recv[s, d] for d in (4, 5)], axis=0)
        if s > 0:
            a = jnp.transpose(came)
            odd = jnp.concatenate([a[5 * PB : 9 * PB, :], a[4 * PB : 5 * PB, :]], axis=0)
            paired = nn(jnp.concatenate(two(jnp.concatenate([a[0 : 5 * PB, :], odd], axis=1)), axis=1), far_pairs)
            for c in range(4):
                for k in range(5):
                    Zp[c * PB : (c + 1) * PB, k * LN : (k + 1) * LN] = paired[k * PB : (k + 1) * PB, c * LN : (c + 1) * LN]
            Sp[...] += nn(PT3[...], stack3(Zp[...]))[0:NM, :]
            horner_fast()
            waiting.append((*turned(came), far_fs))
        else:
            slow_source(0, nn(jnp.concatenate(turned(came), axis=1), far_all))

    def weighted(k, g):
        cols = slice(g * LN, (g + 1) * LN)
        return WK[k, :, cols] + SLOW[0][k] * MF[0, :, cols]

    for base in (0, 3, 6):
        multiply(T9, base, [weighted(TERMS - 1, base + q) for q in range(3)])
    here, there = T9, U9
    stores = [
        pltpu.make_async_copy(o_ref.at[pl.ds(3 * i, 3)], o_out.at[pl.ds(3 * i, 3)], osem.at[i]) for i in range(3)
    ]
    for k in range(TERMS - 2, -1, -1):
        def emit(base, values):
            totals = [values[q] + weighted(k, base + q) for q in range(3)]
            if k > 0:
                multiply(there, base, totals)
            else:
                for q in range(3):
                    o_ref[base + q] += totals[q]
                stores[base // 3].start()

        star_full(here, emit)
        here, there = there, here

    for s in range(STEPS):
        sent_all(s)
    for store in stores:
        store.wait()


def pick_two(a, cm2):
    return jnp.concatenate([pick(a[:, 0:256], cm2), pick(a[:, 256:512], cm2)], axis=1)


def body(
    final_adjoint, star_mats, deriv_stiff, volume_stiffness, face_projection,
    flux_local, flux_across, cluster, partner, send_slots,
):
    V = pltpu.VMEM
    D = pltpu.SemaphoreType.DMA
    views = (
        final_adjoint, jnp.transpose(star_mats, (1, 2, 0, 3)), deriv_stiff, volume_stiffness,
        jnp.transpose(face_projection, (1, 0, 2)), jnp.transpose(flux_local, (1, 2, 0, 3)),
        jnp.transpose(flux_across, (1, 2, 0, 3)), cluster.reshape(1, LN), partner, send_slots,
    )
    scratch = [V(a.shape, a.dtype) for a in views] + [
        D((10,)), V(final_adjoint.shape, F32), D((3,)),
        V((168, 192), B16), V((168, 192), B16), V((96, 192), B16), V((64, 288), B16), V((96, LN), F32), V((168, LN), F32),
        V((192, 1152), B16), V((192, 640), B16), V((168, 1152), F32), V((168, 640), F32), V((96, 1152), F32), V((96, 640), F32),
        V((256, 512), F32), V((256, 256), F32), V((184, LN), F32), V((184, LN), F32),
        V((184, LN), F32), V((184, LN), F32), V((184, LN), F32),
        V((NM, 640), F32), V((NM, 640), F32), V((NM, 1152), F32), V((STEPS, NM, 1152), F32),
        V((96, 1152), F32), V((96, 640), F32), V((168, 640), F32), V((168, 1152), F32), V((TERMS, NM, 1152), F32),
        V((2, 6, 16, 256), F32), V((2, 6, 16, 256), F32),
        V((STEPS - 1, 6, 16, 256), F32), V((STEPS - 1, 6, 16, 256), F32),
        D((2, 6)), D((2, 6)), D((STEPS - 1, 6)), D((STEPS - 1, 6)),
    ]
    return pl.pallas_call(
        kernel,
        out_shape=jax.ShapeDtypeStruct(final_adjoint.shape, F32),
        in_specs=[pl.BlockSpec(memory_space=pltpu.HBM)] * 10,
        out_specs=pl.BlockSpec(memory_space=pltpu.HBM),
        scratch_shapes=scratch,
        compiler_params=pltpu.CompilerParams(collective_id=0, has_side_effects=True, vmem_limit_bytes=64 * 2**20),
        name="coarse_step",
    )(*views)


def solution(mesh):
    every = ("gx", "gy", "gz")
    in_specs = (
        P(None, None, every), P(None, None, None, every), P(), P(), P(),
        P(None, None, None, every), P(None, None, None, every), P(every), P(None, every), P(None, every),
    )
    return jax.shard_map(body, mesh=mesh, in_specs=in_specs, out_specs=P(None, None, every), check_vma=False)
```
